256 devices in a mesh: dp: 4 (over y), row: 4 (over z_lo, core), col: 16 (over x, z_hi).
Axes of the slice: x: 4, y: 4, z: 8 (z_hi: 4, z_lo: 2; z = z_hi * 2 + z_lo), core: 2. Of those that a mesh axis runs over, the one named last changes fastest.
Arguments:
- weight: float32 [512, 73728], P('row', 'col'), may hold values from -6 to 6
- grad_parts: bfloat16 [4, 512, 73728], P('dp', 'row', 'col'), may hold values from -200 to 200
- row_moment: float32 [512], P('row'), may hold values from 0.2 to 20
- col_moment: float32 [73728], P('col'), may hold values from 0.2 to 20
Outputs:
- new_weight: float32 [512, 73728], P('row', 'col')
- update: float32 [512, 73728], P('row', 'col')
- row_new: float32 [512], P('row')
- col_new: float32 [73728], P('col')
- clip_factor: float32 [], replicated
The draws below stay inside these ranges and needn't reach their ends.
All inputs are finite; a program needn't handle non-finite values.
Results may differ from the reference program's by a relative error of at most 0.0003.
Values sent between devices are 32-bit elements; how exact they have to be, the bound alone decides.
A program may use at most 64 MiB of HBM per device.

```python
import math
import jax
import jax.numpy as jnp
from jax import lax

FF = 73728
ROWS = 512
N_DP = 4


def draw_grad_parts(key, part):
    key = jax.random.fold_in(key, 11)
    keys = jax.random.split(key, 7)
    place = jnp.arange(ROWS, dtype=jnp.float32).reshape(1, ROWS, 1) / (ROWS - 1.0)
    rise = jnp.exp(place * jnp.log(4.0))
    rough = jnp.exp(jax.random.uniform(keys[0], (1, ROWS, 1), jnp.float32, 0.0, jnp.log(2.0)))
    row_scale = rise * rough
    col_scale = jnp.exp(jax.random.uniform(keys[1], (1, 1, FF), jnp.float32, jnp.log(0.25), 0.0))
    rep_scale = jnp.exp(jax.random.uniform(keys[2], (N_DP, 1, 1), jnp.float32, 0.0, jnp.log(3.0)))
    hot_rows = jax.random.randint(keys[5], (1, ROWS, 1), 0, 2).astype(jnp.float32)
    hot_cols = jax.random.randint(keys[6], (1, 1, FF), 0, 2).astype(jnp.float32)
    boost = jnp.exp(0.7 * hot_rows * hot_cols)
    noise = jnp.clip(jax.random.normal(keys[3], (N_DP, ROWS, FF), jnp.float32), -4.0, 4.0)
    return (noise * row_scale * col_scale * rep_scale * boost).astype(jnp.bfloat16)


def level_of(rng, dims, cuts, least, high):
    level, own = 1.0, jax.random.fold_in(rng, 6)
    for axis_at, shards_of in cuts:
        steps = jnp.exp(jax.random.uniform(jax.random.fold_in(own, axis_at), (shards_of,), jnp.float32, least / len(cuts), high / len(cuts)))
        level = level * jnp.repeat(steps, dims[axis_at] // shards_of).reshape([-1 if axis == axis_at else 1 for axis in range(len(dims))])
    return level


def scatter_about(stream_key, shape, spread, bound, shards=(), kind=jnp.bfloat16):
    entries = spread * jax.random.normal(stream_key, shape, jnp.float32)
    if shards:
        entries = entries * level_of(stream_key, shape, shards, -0.22, 0.18)
    return jnp.clip(entries, -bound, bound).astype(kind)


def setup_inputs(seed: int = 0) -> dict:
    seeds = jax.random.split(jax.random.key(seed), 5)
    return {
        "weight": scatter_about(seeds[0], (ROWS, FF), 1.0, 6.0, ((0, 4), (1, 16)), jnp.float32),
        "grad_parts": draw_grad_parts(jax.random.fold_in(seeds[4], 71), 0),
        "row_moment": jnp.clip(jnp.exp(math.log(20.0) - 4.6051702 * jax.random.uniform(seeds[2], (ROWS,), jnp.float32) ** level_of(seeds[2], (ROWS,), ((0, 4),), -0.2, 0.2)), 0.2, 20.0),
        "col_moment": jnp.clip(jnp.exp(math.log(20.0) - 4.6051702 * jax.random.uniform(seeds[3], (FF,), jnp.float32) ** level_of(seeds[3], (FF,), ((0, 16),), -0.2, 0.2)), 0.2, 20.0),
    }


decay_rate = 0.5
eps_one = 1e-30
eps_two = 0.001
learn_rate = 0.01
clip_level = 1.0

def reference(weight, grad_parts, row_moment, col_moment):
    grad = lax.optimization_barrier(jnp.sum(grad_parts.astype(jnp.float32), axis=0))
    squared = grad * grad
    row_new = decay_rate * row_moment + (1.0 - decay_rate) * (lax.optimization_barrier(jnp.mean(squared, axis=1)) + eps_one)
    col_new = decay_rate * col_moment + (1.0 - decay_rate) * (lax.optimization_barrier(jnp.mean(squared, axis=0)) + eps_one)
    row_mean = jnp.mean(row_new)
    raw = grad / jnp.sqrt(row_new[:, None] * col_new[None, :] / row_mean)
    clip = jnp.maximum(1.0, jnp.sqrt(jnp.mean(raw * raw)) / clip_level)
    update = raw / clip
    step_size = learn_rate * jnp.maximum(eps_two, jnp.sqrt(jnp.mean(weight * weight)))
    new_weight = weight - step_size * update
    return (new_weight, update, row_new, col_new, clip)
```

```python
import functools

import jax
import jax.numpy as jnp
from jax import lax
from jax.experimental import pallas as pl
from jax.experimental.pallas import tpu as pltpu
from jax.sharding import PartitionSpec as P

decay_rate = 0.5
eps_one = 1e-30
eps_two = 0.001
learn_rate = 0.01
clip_level = 1.0

MESH = pl.DeviceIdType.MESH
f32 = jnp.float32
CHUNKS = 4
PA, PB, PC, PD, PX, PE = range(6)


def exchange_kernel(sizes, grad_hbm, weight_hbm, rowm_hbm, colm_hbm,
                    full, held, col_all, row_new, row_scale, col_scale, scal,
                    own, s_opp, s_right, s_left, r_opp, r_left, r_right, lanes,
                    rowm, colm, col_old, col_parts, row_parts, scal_parts,
                    load_sem, send_sem, recv_sem, xs_sem, xr_sem, cs_sem, cr_sem):
    n_dp, n_row, n_col, splits = sizes
    rows, width = own.shape[1], own.shape[2]
    half = rows // 2
    step = half // CHUNKS
    rows_all = rows * n_row
    cols_all = width * n_dp * n_col
    entries = float(rows_all) * float(cols_all)
    y, r, c = lax.axis_index("dp"), lax.axis_index("row"), lax.axis_index("col")
    right, opp, left = lax.rem(y + 1, 4), lax.rem(y + 2, 4), lax.rem(y + 3, 4)

    groups = [("dp", y, n_dp, lambda i: i)]
    for size, stride in splits:
        at = lax.rem(c // stride, size)
        groups.append(("col", at, size, functools.partial(lambda s, a, i: c + (i - a) * s, stride, at)))
    row_group = ("row", r, n_row, lambda i: i)

    def peers(group):
        axis, at, size, index = group
        return [(d, {axis: index(lax.rem(at + d, size))}, lax.rem(at + size - d, size)) for d in range(1, size)]

    loads = {}
    for slot, q in ((2, opp), (1, right), (3, left), (0, y)):
        loads[slot] = pltpu.make_async_copy(
            grad_hbm.at[0, :, pl.ds(pl.multiple_of(q * width, 128), width)], own.at[slot], load_sem.at[slot])
        loads[slot].start()
    barrier = pltpu.get_barrier_semaphore()
    count = 0
    for group in groups + [row_group]:
        for _, dev, _ in peers(group):
            pl.semaphore_signal(barrier, inc=1, device_id=dev, device_id_type=MESH)
            count += 1
    wloads = []
    for q in range(4):
        wloads.append(pltpu.make_async_copy(
            weight_hbm.at[:, pl.ds(q * width, width)], held.at[q], load_sem.at[4 + q]))
        wloads[-1].start()
    load_row = pltpu.make_async_copy(rowm_hbm, rowm, load_sem.at[8])
    load_col = pltpu.make_async_copy(colm_hbm, colm, load_sem.at[9])
    load_row.start()
    load_col.start()

    def at(h, k):
        return pl.ds(h * half + k * step, step)

    def bulk(phase, d, k):
        if phase == PA:
            src, dst = s_opp.at[at(d, k)], r_opp.at[at(d, k)]
        elif phase in (PB, PC):
            h = d if phase == PC else 1 - d
            src, dst = ((s_right, r_left), (s_left, r_right))[d]
            src, dst = src.at[at(h, k)], dst.at[at(h, k)]
        else:
            h = 1 - d if phase == PX else d
            q = y if phase != PE else (left, right)[d]
            src = dst = full.at[q, at(h, k)]
        return pltpu.make_async_remote_copy(
            src_ref=src, dst_ref=dst, send_sem=send_sem.at[phase, d, k], recv_sem=recv_sem.at[phase, d, k],
            device_id={"dp": (right, left)[d]}, device_id_type=MESH)

    def arrive(phase, d, k):
        if phase < PD:
            bulk(phase, d, k).wait_recv()
            return
        h = 1 - d if phase == PX else d
        q = (left, right)[d] if phase != PE else opp
        ref = full.at[q, at(h, k)]
        pltpu.make_async_remote_copy(
            src_ref=ref, dst_ref=ref, send_sem=send_sem.at[phase, d, k], recv_sem=recv_sem.at[phase, d, k],
            device_id={"dp": (right, left)[d]}, device_id_type=MESH).wait_recv()

    loads[2].wait()
    for k in range(CHUNKS):
        for d in range(2):
            s_opp[at(d, k)] = own[2, at(d, k)].astype(f32)
    pl.semaphore_wait(barrier, count)
    for k in range(CHUNKS):
        for d in range(2):
            bulk(PA, d, k).start()
    loads[1].wait()
    loads[3].wait()
    for k in range(CHUNKS):
        for d, (dst, slot) in enumerate(((s_right, 1), (s_left, 3))):
            dst[at(1 - d, k)] = own[slot, at(1 - d, k)].astype(f32)
            bulk(PB, d, k).start()
    for copy in wloads:
        copy.wait()

    def weight_step(i, acc):
        w = held[y, pl.ds(pl.multiple_of(i * 8, 8), 8)]
        sq = w * w
        for j in range(width // 128):
            acc = acc + sq[:, j * 128:(j + 1) * 128]
        return acc

    w_lanes = lax.fori_loop(0, rows // 8, weight_step, jnp.zeros((8, 128), f32))
    for k in range(CHUNKS):
        for d, (dst, slot) in enumerate(((s_right, 1), (s_left, 3))):
            arrive(PA, d, k)
            dst[at(d, k)] = r_opp[at(d, k)] + own[slot, at(d, k)].astype(f32)
            bulk(PC, d, k).start()
    loads[0].wait()
    col_acc = jnp.zeros((8, width), f32)
    for k in range(CHUNKS):
        for d in range(2):
            arrive(PB, 1 - d, k)
            arrive(PC, d, k)
            g = own[0, at(d, k)].astype(f32) + r_left[at(d, k)] + r_right[at(d, k)]
            full[y, at(d, k)] = g
            bulk(PD, d, k).start()
            bulk(PX, 1 - d, k).start()
            sq = g * g
            for i in range(step // 8):
                col_acc = col_acc + sq[i * 8:(i + 1) * 8]
            part = sq[:, :128]
            for j in range(1, width // 128):
                part = part + sq[:, j * 128:(j + 1) * 128]
            lanes[at(d, k)] = part

    def send_small(stage, group, parts, own_slot):
        copies = []
        for d, dev, _ in peers(group):
            copies.append(pltpu.make_async_remote_copy(
                src_ref=parts.at[own_slot], dst_ref=parts.at[own_slot], send_sem=xs_sem.at[stage, d - 1],
                recv_sem=xr_sem.at[stage, d - 1], device_id=dev, device_id_type=MESH))
            copies[-1].start()
        return copies

    def wait_small(stage, group, parts):
        for d, dev, sender in peers(group):
            pltpu.make_async_remote_copy(
                src_ref=parts.at[sender], dst_ref=parts.at[sender], send_sem=xs_sem.at[stage, d - 1],
                recv_sem=xr_sem.at[stage, d - 1], device_id=dev, device_id_type=MESH).wait_recv()

    def total(parts, size):
        out = parts[0]
        for i in range(1, size):
            out = out + parts[i]
        return out

    pending = []
    stage = 0
    col_parts[r] = jnp.sum(col_acc, axis=0, keepdims=True)
    pending += send_small(stage, row_group, col_parts, r)
    value = jnp.sum(lanes[...].T, axis=0, keepdims=True)
    forwards = [(k, d) for k in range(CHUNKS) for d in range(2)]

    def forward(n):
        for _ in range(n):
            if forwards:
                k, d = forwards.pop(0)
                arrive(PD, d, k)
                bulk(PE, d, k).start()

    row_stages = []
    for i, group in enumerate(groups):
        stage += 1
        parts = row_parts.at[i]
        parts[group[1]] = value
        pending += send_small(stage, group, parts, group[1])
        if i == 0:
            wait_small(0, row_group, col_parts)
            load_col.wait()
            span = pl.ds(pl.multiple_of(y * width, 128), width)
            col_old[...] = colm[...].reshape(col_old.shape)
            mine = decay_rate * col_old[:, span] + (1.0 - decay_rate) * (total(col_parts, n_row) / rows_all + eps_one)
            col_all[:, span] = mine
            for d, dev, _ in peers(groups[0]):
                copy = pltpu.make_async_remote_copy(
                    src_ref=col_all.at[:, span], dst_ref=col_all.at[:, span], send_sem=cs_sem.at[d - 1],
                    recv_sem=cr_sem.at[d - 1], device_id=dev, device_id_type=MESH)
                copy.start()
                pending.append(copy)
            inverse = 1.0 / mine

            def raw_step(k, _):
                at_k = pl.ds(pl.multiple_of(k * 8, 8), 8)
                g = full[y, at_k]
                sq = g * g * inverse
                part = sq[:, :128]
                for j in range(1, width // 128):
                    part = part + sq[:, j * 128:(j + 1) * 128]
                lanes[at_k] = part
                return 0

            lax.fori_loop(0, rows // 8, raw_step, 0)
            raw_cols = jnp.sum(lanes[...].T, axis=0, keepdims=True)
        forward(1)
        wait_small(stage, group, parts)
        value = total(parts, group[2])
    load_row.wait()
    mine = decay_rate * rowm[...].reshape(1, rows) + (1.0 - decay_rate) * (value / cols_all + eps_one)
    row_new[...] = mine
    tile = jnp.concatenate([
        raw_cols / mine,
        mine * (1.0 / (n_dp * n_col)),
        jnp.sum(w_lanes, axis=0, keepdims=True),
        jnp.zeros((5, 128), f32)], axis=0)
    for i, group in enumerate(groups + [row_group]):
        stage += 1
        parts = scal_parts.at[i]
        parts[group[1]] = tile
        pending += send_small(stage, group, parts, group[1])
        forward(2)
        wait_small(stage, group, parts)
        tile = total(parts, group[2])
    forward(len(forwards))
    sums = jnp.sum(tile, axis=1, keepdims=True)
    row_mean = sums[1:2] / rows_all
    clip = jnp.maximum(1.0, jnp.sqrt(sums[0:1] * row_mean / entries) / clip_level)
    size = learn_rate * jnp.maximum(eps_two, jnp.sqrt(sums[2:3] / entries))
    scal[...] = jnp.concatenate([jnp.broadcast_to(clip, (1, 128)), jnp.broadcast_to(size, (1, 128))], axis=0)
    scale = lax.rsqrt(mine) * (jnp.sqrt(row_mean) / clip)
    row_scale[...] = jnp.broadcast_to(scale, (128, 128)).T
    for d, dev, sender in peers(groups[0]):
        ref = col_all.at[:, pl.ds(pl.multiple_of(sender * width, 128), width)]
        pltpu.make_async_remote_copy(
            src_ref=ref, dst_ref=ref, send_sem=cs_sem.at[d - 1], recv_sem=cr_sem.at[d - 1],
            device_id=dev, device_id_type=MESH).wait_recv()
    col_scale[...] = lax.rsqrt(col_all[...])
    for k in range(CHUNKS):
        for d in range(2):
            arrive(PX, d, k)
            arrive(PE, d, k)
    for copy in pending:
        copy.wait_send()
    for phase in range(6):
        for k in range(CHUNKS):
            for d in range(2):
                bulk(phase, d, k).wait_send()


def update_kernel(full, held, col_all, row_new, row_scale, col_scale, scal,
                  weight_out, update_out, row_out, col_out, clip_out,
                  new_weight, update, sem):
    rows, width = full.shape[1], full.shape[2]
    size = scal[1:2, :]
    step = 32
    copies = []
    for q in range(4):
        for k in range(rows // step):
            for i in range(step // 8):
                at = pl.ds(k * step + i * 8, 8)
                by_row = row_scale[at]
                for j in range(width // 128):
                    col = pl.ds(j * 128, 128)
                    u = full[q, at, col] * by_row * col_scale[:, pl.ds(q * width + j * 128, 128)]
                    update[q, at, col] = u
                    new_weight[q, at, col] = held[q, at, col] - size * u
            at = pl.ds(k * step, step)
            for which, (src, dst) in enumerate(((update, update_out), (new_weight, weight_out))):
                copies.append(pltpu.make_async_copy(
                    src.at[q, at], dst.at[at, pl.ds(q * width, width)], sem.at[which, q, k]))
                copies[-1].start()
    row_out[...] = row_new[...].reshape(row_out.shape)
    col_out[...] = col_all[...].reshape(col_out.shape)
    clip_out[...] = scal[0:1, 0:1]
    for copy in copies:
        copy.wait()


def solution(mesh):
    n_dp, n_row, n_col = mesh.shape["dp"], mesh.shape["row"], mesh.shape["col"]
    splits = ((4, 4), (4, 1)) if n_col == 16 else ((n_col, 1),)
    sizes = (n_dp, n_row, n_col, splits)

    def body(weight, grad_parts, row_moment, col_moment):
        rows, cols = weight.shape
        width = cols // n_dp
        vmem = pl.BlockSpec(memory_space=pltpu.VMEM)
        hbm = pl.BlockSpec(memory_space=pltpu.HBM)
        shapes = ((4, rows, width), (4, rows, width), (1, cols), (1, rows), (rows, 128), (1, cols), (2, 128))
        n_groups = 2 + len(splits)
        most = max(n_dp, n_row, *(s for s, _ in splits))
        stages = 1 + (n_groups - 1) + n_groups
        outs = pl.pallas_call(
            functools.partial(exchange_kernel, sizes),
            out_shape=tuple(pltpu.VMEM(s, f32) for s in shapes),
            in_specs=[hbm] * 4,
            out_specs=(vmem,) * len(shapes),
            scratch_shapes=[
                pltpu.VMEM((4, rows, width), jnp.bfloat16),
                *[pltpu.VMEM((rows, width), f32) for _ in range(6)],
                pltpu.VMEM((rows, 128), f32),
                pltpu.VMEM((rows,), f32),
                pltpu.VMEM((cols,), f32),
                pltpu.VMEM((1, cols), f32),
                pltpu.VMEM((n_row, 1, width), f32),
                pltpu.VMEM((n_groups - 1, most, 1, rows), f32),
                pltpu.VMEM((n_groups, most, 8, 128), f32),
                pltpu.SemaphoreType.DMA((10,)),
                pltpu.SemaphoreType.DMA((6, 2, CHUNKS)),
                pltpu.SemaphoreType.DMA((6, 2, CHUNKS)),
                pltpu.SemaphoreType.DMA((stages, most - 1)),
                pltpu.SemaphoreType.DMA((stages, most - 1)),
                pltpu.SemaphoreType.DMA((3,)),
                pltpu.SemaphoreType.DMA((3,)),
            ],
            compiler_params=pltpu.CompilerParams(
                collective_id=0, has_side_effects=True, vmem_limit_bytes=24 << 20),
            name="exchange",
        )(*(pltpu.with_memory_space_constraint(a, pltpu.HBM) for a in (grad_parts, weight, row_moment, col_moment)))
        new_weight, update, row_new, col_new, clip = pl.pallas_call(
            update_kernel,
            out_shape=(
                jax.ShapeDtypeStruct((rows, cols), f32),
                jax.ShapeDtypeStruct((rows, cols), f32),
                jax.ShapeDtypeStruct((rows,), f32),
                jax.ShapeDtypeStruct((cols,), f32),
                jax.ShapeDtypeStruct((1, 1), f32),
            ),
            in_specs=[vmem] * len(shapes),
            out_specs=(pl.BlockSpec(memory_space=pl.ANY), pl.BlockSpec(memory_space=pl.ANY), vmem, vmem, vmem),
            scratch_shapes=[
                pltpu.VMEM((4, rows, width), f32),
                pltpu.VMEM((4, rows, width), f32),
                pltpu.SemaphoreType.DMA((2, 4, rows // 32)),
            ],
            compiler_params=pltpu.CompilerParams(vmem_limit_bytes=24 << 20),
            name="apply",
        )(*outs)
        return new_weight, update, row_new, col_new, clip.reshape(())

    return jax.shard_map(
        body,
        mesh=mesh,
        in_specs=(P("row", "col"), P("dp", "row", "col"), P("row"), P("col")),
        out_specs=(P("row", "col"), P("row", "col"), P("row"), P("col"), P()),
        check_vma=False,
    )
```

```python
import functools

import jax
import jax.numpy as jnp
from jax import lax
from jax.experimental import pallas as pl
from jax.experimental.pallas import tpu as pltpu
from jax.sharding import PartitionSpec as P

decay_rate = 0.5
eps_one = 1e-30
eps_two = 0.001
learn_rate = 0.01
clip_level = 1.0

MESH = pl.DeviceIdType.MESH
f32 = jnp.float32
CHUNKS = 4
PA, PB, PC, PD, PX, PE = range(6)


def exchange_kernel(sizes, grad_hbm, weight_hbm, rowm_hbm, colm_hbm,
                    full, held, col_all, row_new, row_scale, col_scale, scal,
                    own, s_opp, s_right, s_left, r_opp, r_left, r_right, lanes,
                    rowm, colm, col_old, col_parts, sums_col, sums_dp, sums_row,
                    load_sem, send_sem, recv_sem, xs_sem, xr_sem):
    n_dp, n_row, n_col = sizes
    rows, width = own.shape[1], own.shape[2]
    half = rows // 2
    step = half // CHUNKS
    rows_all = rows * n_row
    cols_all = width * n_dp * n_col
    entries = float(rows_all) * float(cols_all)
    y, r, c = lax.axis_index("dp"), lax.axis_index("row"), lax.axis_index("col")
    right, opp, left = lax.rem(y + 1, 4), lax.rem(y + 2, 4), lax.rem(y + 3, 4)

    dp_group, row_group, col_group = ("dp", y, n_dp), ("row", r, n_row), ("col", c, n_col)

    def peers(group):
        axis, at, size = group
        return [{axis: lax.rem(at + d, size)} for d in range(1, size)]

    loads = {}
    for slot, q in ((2, opp), (1, right), (3, left), (0, y)):
        loads[slot] = pltpu.make_async_copy(
            grad_hbm.at[0, :, pl.ds(pl.multiple_of(q * width, 128), width)], own.at[slot], load_sem.at[slot])
        loads[slot].start()
    barrier = pltpu.get_barrier_semaphore()
    count = 0
    for group in (dp_group, row_group, col_group):
        for dev in peers(group):
            pl.semaphore_signal(barrier, inc=1, device_id=dev, device_id_type=MESH)
            count += 1
    wloads = []
    for q in range(4):
        wloads.append(pltpu.make_async_copy(
            weight_hbm.at[:, pl.ds(q * width, width)], held.at[q], load_sem.at[4 + q]))
        wloads[-1].start()
    load_row = pltpu.make_async_copy(rowm_hbm, rowm, load_sem.at[8])
    load_col = pltpu.make_async_copy(colm_hbm, colm, load_sem.at[9])
    load_row.start()
    load_col.start()

    def at(h, k):
        return pl.ds(h * half + k * step, step)

    def bulk(phase, d, k):
        if phase == PA:
            src, dst = s_opp.at[at(d, k)], r_opp.at[at(d, k)]
        elif phase in (PB, PC):
            h = d if phase == PC else 1 - d
            src, dst = ((s_right, r_left), (s_left, r_right))[d]
            src, dst = src.at[at(h, k)], dst.at[at(h, k)]
        else:
            h = 1 - d if phase == PX else d
            q = y if phase != PE else (left, right)[d]
            src = dst = full.at[q, at(h, k)]
        return pltpu.make_async_remote_copy(
            src_ref=src, dst_ref=dst, send_sem=send_sem.at[phase, d, k], recv_sem=recv_sem.at[phase, d, k],
            device_id={"dp": (right, left)[d]}, device_id_type=MESH)

    def arrive(phase, d, k):
        if phase < PD:
            bulk(phase, d, k).wait_recv()
            return
        h = 1 - d if phase == PX else d
        q = (left, right)[d] if phase != PE else opp
        ref = full.at[q, at(h, k)]
        pltpu.make_async_remote_copy(
            src_ref=ref, dst_ref=ref, send_sem=send_sem.at[phase, d, k], recv_sem=recv_sem.at[phase, d, k],
            device_id={"dp": (right, left)[d]}, device_id_type=MESH).wait_recv()

    loads[2].wait()
    for k in range(CHUNKS):
        for d in range(2):
            s_opp[at(d, k)] = own[2, at(d, k)].astype(f32)
    pl.semaphore_wait(barrier, count)
    for k in range(CHUNKS):
        for d in range(2):
            bulk(PA, d, k).start()
    loads[1].wait()
    loads[3].wait()
    for k in range(CHUNKS):
        for d, (dst, slot) in enumerate(((s_right, 1), (s_left, 3))):
            dst[at(1 - d, k)] = own[slot, at(1 - d, k)].astype(f32)
            bulk(PB, d, k).start()
    for copy in wloads:
        copy.wait()

    def weight_step(i, acc):
        w = held[y, pl.ds(pl.multiple_of(i * 8, 8), 8)]
        sq = w * w
        for j in range(width // 128):
            acc = acc + sq[:, j * 128:(j + 1) * 128]
        return acc

    w_lanes = lax.fori_loop(0, rows // 8, weight_step, jnp.zeros((8, 128), f32))
    for k in range(CHUNKS):
        for d, (dst, slot) in enumerate(((s_right, 1), (s_left, 3))):
            arrive(PA, d, k)
            dst[at(d, k)] = r_opp[at(d, k)] + own[slot, at(d, k)].astype(f32)
            bulk(PC, d, k).start()
    loads[0].wait()
    col_acc = jnp.zeros((8, width), f32)
    for k in range(CHUNKS):
        for d in range(2):
            arrive(PB, 1 - d, k)
            arrive(PC, d, k)
            g = own[0, at(d, k)].astype(f32) + r_left[at(d, k)] + r_right[at(d, k)]
            full[y, at(d, k)] = g
            bulk(PD, d, k).start()
            bulk(PX, 1 - d, k).start()
            sq = g * g
            for i in range(step // 8):
                col_acc = col_acc + sq[i * 8:(i + 1) * 8]
            part = sq[:, :128]
            for j in range(1, width // 128):
                part = part + sq[:, j * 128:(j + 1) * 128]
            lanes[at(d, k)] = part

    def send_small(stage, group, parts):
        mine = parts.at[group[1]]
        copies = []
        for dev in peers(group):
            copies.append(pltpu.make_async_remote_copy(
                src_ref=mine, dst_ref=mine, send_sem=xs_sem.at[stage], recv_sem=xr_sem.at[stage],
                device_id=dev, device_id_type=MESH))
            copies[-1].start()

    def all_but_one(stage, group, parts):
        rest = parts.at[pl.ds(0, group[2] - 1)]
        return pltpu.make_async_remote_copy(
            src_ref=rest, dst_ref=rest, send_sem=xs_sem.at[stage], recv_sem=xr_sem.at[stage],
            device_id=peers(group)[0], device_id_type=MESH)

    def total(parts):
        out = parts[0]
        for i in range(1, parts.shape[0]):
            out = out + parts[i]
        return out

    col_parts[r] = jnp.sum(col_acc, axis=0, keepdims=True)
    send_small(0, row_group, col_parts)
    row_sums = jnp.sum(lanes[...].T, axis=0, keepdims=True)
    weight_sums = jnp.sum(w_lanes, axis=0, keepdims=True)
    load_col.wait()
    col_old[...] = colm[...].reshape(col_old.shape)
    span = pl.ds(pl.multiple_of(y * width, 128), width)
    old = col_old[:, span]
    all_but_one(0, row_group, col_parts).wait_recv()
    col_mine = decay_rate * old + (1.0 - decay_rate) * (total(col_parts) / rows_all + eps_one)
    inverse = 1.0 / col_mine

    def raw_step(k, _):
        at_k = pl.ds(pl.multiple_of(k * 8, 8), 8)
        g = full[y, at_k]
        sq = g * g * inverse
        part = sq[:, :128]
        for j in range(1, width // 128):
            part = part + sq[:, j * 128:(j + 1) * 128]
        lanes[at_k] = part
        return 0

    lax.fori_loop(0, rows // 8, raw_step, 0, unroll=4)
    raw_sums = jnp.sum(lanes[...].T, axis=0, keepdims=True)
    sums_col[c] = jnp.concatenate([row_sums, raw_sums, weight_sums, jnp.zeros((5, 128), f32)], axis=0)
    send_small(1, col_group, sums_col)
    col_all[:, span] = col_mine
    for dev in peers(dp_group):
        pltpu.make_async_remote_copy(
            src_ref=col_all.at[:, span], dst_ref=col_all.at[:, span], send_sem=xs_sem.at[4],
            recv_sem=xr_sem.at[4], device_id=dev, device_id_type=MESH).start()
    load_row.wait()
    all_but_one(1, col_group, sums_col).wait_recv()
    sums_dp[y] = total(sums_col)
    send_small(2, dp_group, sums_dp)
    for k in range(CHUNKS):
        for d in range(2):
            arrive(PD, d, k)
            bulk(PE, d, k).start()
    all_but_one(2, dp_group, sums_dp).wait_recv()
    tile = total(sums_dp)
    row_mine = decay_rate * rowm[...].reshape(1, rows) + (1.0 - decay_rate) * (tile[0:1] / cols_all + eps_one)
    row_new[...] = row_mine
    sums_row[r] = jnp.concatenate([tile[1:2] / row_mine, row_mine, tile[2:3], jnp.zeros((5, 128), f32)], axis=0)
    send_small(3, row_group, sums_row)
    cols_rest = col_all.at[:, pl.ds(0, 3 * width)]
    col_round = pltpu.make_async_remote_copy(
        src_ref=cols_rest, dst_ref=cols_rest, send_sem=xs_sem.at[4], recv_sem=xr_sem.at[4],
        device_id=peers(dp_group)[0], device_id_type=MESH)
    col_round.wait_recv()
    col_scale[...] = lax.rsqrt(col_all[...])
    all_but_one(3, row_group, sums_row).wait_recv()
    sums = jnp.sum(total(sums_row), axis=1, keepdims=True)
    row_mean = sums[1:2] / rows_all
    clip = jnp.maximum(1.0, jnp.sqrt(sums[0:1] * row_mean / entries) / clip_level)
    size = learn_rate * jnp.maximum(eps_two, jnp.sqrt(sums[2:3] / entries))
    scal[...] = jnp.concatenate([jnp.broadcast_to(clip, (1, 128)), jnp.broadcast_to(size, (1, 128))], axis=0)
    scale = lax.rsqrt(row_mine) * (jnp.sqrt(row_mean) / clip)
    row_scale[...] = jnp.broadcast_to(scale, (128, 128)).T
    for k in range(CHUNKS):
        for d in range(2):
            arrive(PX, d, k)
            arrive(PE, d, k)
    for stage, (group, parts) in enumerate(
            ((row_group, col_parts), (col_group, sums_col), (dp_group, sums_dp), (row_group, sums_row))):
        all_but_one(stage, group, parts).wait_send()
    col_round.wait_send()
    for phase in range(6):
        for k in range(CHUNKS):
            for d in range(2):
                bulk(phase, d, k).wait_send()


def update_kernel(full, held, col_all, row_new, row_scale, col_scale, scal,
                  weight_out, update_out, row_out, col_out, clip_out,
                  new_weight, update, sem):
    rows, width = full.shape[1], full.shape[2]
    size = scal[1:2, :]
    step = 16
    copies = []
    for k in range(rows // step):
        for i in range(step // 8):
            at = pl.ds(k * step + i * 8, 8)
            by_row = row_scale[at]
            for q in range(4):
                for j in range(width // 128):
                    col = pl.ds(j * 128, 128)
                    out = pl.ds(q * width + j * 128, 128)
                    u = full[q, at, col] * by_row * col_scale[:, out]
                    update[at, out] = u
                    new_weight[at, out] = held[q, at, col] - size * u
        at = pl.ds(k * step, step)
        for which, (src, dst) in enumerate(((update, update_out), (new_weight, weight_out))):
            copies.append(pltpu.make_async_copy(src.at[at], dst.at[at], sem.at[which, k]))
            copies[-1].start()
    row_out[...] = row_new[...].reshape(row_out.shape)
    col_out[...] = col_all[...].reshape(col_out.shape)
    clip_out[...] = scal[0:1, 0:1]
    for copy in copies:
        copy.wait()


def solution(mesh):
    n_dp, n_row, n_col = mesh.shape["dp"], mesh.shape["row"], mesh.shape["col"]
    sizes = (n_dp, n_row, n_col)

    def body(weight, grad_parts, row_moment, col_moment):
        rows, cols = weight.shape
        width = cols // n_dp
        vmem = pl.BlockSpec(memory_space=pltpu.VMEM)
        hbm = pl.BlockSpec(memory_space=pltpu.HBM)
        shapes = ((4, rows, width), (4, rows, width), (1, cols), (1, rows), (rows, 128), (1, cols), (2, 128))
        outs = pl.pallas_call(
            functools.partial(exchange_kernel, sizes),
            out_shape=tuple(pltpu.VMEM(s, f32) for s in shapes),
            in_specs=[hbm] * 4,
            out_specs=(vmem,) * len(shapes),
            scratch_shapes=[
                pltpu.VMEM((4, rows, width), jnp.bfloat16),
                *[pltpu.VMEM((rows, width), f32) for _ in range(6)],
                pltpu.VMEM((rows, 128), f32),
                pltpu.VMEM((rows,), f32),
                pltpu.VMEM((cols,), f32),
                pltpu.VMEM((1, cols), f32),
                pltpu.VMEM((n_row, 1, width), f32),
                pltpu.VMEM((n_col, 8, 128), f32),
                pltpu.VMEM((n_dp, 8, 128), f32),
                pltpu.VMEM((n_row, 8, 128), f32),
                pltpu.SemaphoreType.DMA((10,)),
                pltpu.SemaphoreType.DMA((6, 2, CHUNKS)),
                pltpu.SemaphoreType.DMA((6, 2, CHUNKS)),
                pltpu.SemaphoreType.DMA((5,)),
                pltpu.SemaphoreType.DMA((5,)),
            ],
            compiler_params=pltpu.CompilerParams(
                collective_id=0, has_side_effects=True, vmem_limit_bytes=24 << 20),
            name="exchange",
        )(*(pltpu.with_memory_space_constraint(a, pltpu.HBM) for a in (grad_parts, weight, row_moment, col_moment)))
        new_weight, update, row_new, col_new, clip = pl.pallas_call(
            update_kernel,
            out_shape=(
                jax.ShapeDtypeStruct((rows, cols), f32),
                jax.ShapeDtypeStruct((rows, cols), f32),
                jax.ShapeDtypeStruct((rows,), f32),
                jax.ShapeDtypeStruct((cols,), f32),
                jax.ShapeDtypeStruct((1, 1), f32),
            ),
            in_specs=[vmem] * len(shapes),
            out_specs=(pl.BlockSpec(memory_space=pl.ANY), pl.BlockSpec(memory_space=pl.ANY), vmem, vmem, vmem),
            scratch_shapes=[
                pltpu.VMEM((rows, cols), f32),
                pltpu.VMEM((rows, cols), f32),
                pltpu.SemaphoreType.DMA((2, rows // 16)),
            ],
            compiler_params=pltpu.CompilerParams(vmem_limit_bytes=24 << 20),
            name="apply",
        )(*outs)
        return new_weight, update, row_new, col_new, clip.reshape(())

    return jax.shard_map(
        body,
        mesh=mesh,
        in_specs=(P("row", "col"), P("dp", "row", "col"), P("row"), P("col")),
        out_specs=(P("row", "col"), P("row", "col"), P("row"), P("col"), P()),
        check_vma=False,
    )
```

```python
import functools

import jax
import jax.numpy as jnp
from jax import lax
from jax.experimental import pallas as pl
from jax.experimental.pallas import tpu as pltpu
from jax.sharding import PartitionSpec as P

decay_rate = 0.5
eps_one = 1e-30
eps_two = 0.001
learn_rate = 0.01
clip_level = 1.0

MESH = pl.DeviceIdType.MESH
f32 = jnp.float32
CHUNKS = 4
PA, PB, PC, PD, PX, PE = range(6)


def exchange_kernel(sizes, grad_hbm, weight_hbm, rowm_hbm, colm_hbm,
                    full, held, col_all, row_new, row_scale, col_scale, scal,
                    own, s_opp, s_right, s_left, r_opp, r_left, r_right, lanes,
                    rowm, colm, col_old, col_parts, sums_col, sums_dp, sums_row,
                    load_sem, send_sem, recv_sem, xs_sem, xr_sem, ready):
    n_dp, n_row, n_col = sizes
    rows, width = own.shape[1], own.shape[2]
    half = rows // 2
    step = half // CHUNKS
    rows_all = rows * n_row
    cols_all = width * n_dp * n_col
    entries = float(rows_all) * float(cols_all)
    y, r, c = lax.axis_index("dp"), lax.axis_index("row"), lax.axis_index("col")
    right, opp, left = lax.rem(y + 1, 4), lax.rem(y + 2, 4), lax.rem(y + 3, 4)

    dp_group, row_group, col_group = ("dp", y, n_dp), ("row", r, n_row), ("col", c, n_col)

    def peers(group):
        axis, at, size = group
        return [{axis: lax.rem(at + d, size)} for d in range(1, size)]

    loads = {}
    for slot, q in ((2, opp), (1, right), (3, left), (0, y)):
        loads[slot] = pltpu.make_async_copy(
            grad_hbm.at[0, :, pl.ds(pl.multiple_of(q * width, 128), width)], own.at[slot], load_sem.at[slot])
    for q in range(4):
        loads[4 + q] = pltpu.make_async_copy(
            weight_hbm.at[:, pl.ds(q * width, width)], held.at[q], load_sem.at[4 + q])
    loads[8] = pltpu.make_async_copy(rowm_hbm, rowm, load_sem.at[8])
    loads[9] = pltpu.make_async_copy(colm_hbm, colm, load_sem.at[9])
    loads[2].start()
    barrier = pltpu.get_barrier_semaphore()
    place = lax.rem(c, 4) * (n_col // 4) + c // 4
    for dev in peers(dp_group):
        pl.semaphore_signal(barrier, inc=1, device_id=dev, device_id_type=MESH)
    for d in range(1, n_col):
        peer = lax.rem(c + d, n_col)

        @pl.when(lax.rem(peer, 4) * (n_col // 4) + peer // 4 > place)
        def _():
            pl.semaphore_signal(barrier, inc=1, device_id={"col": peer}, device_id_type=MESH)

    for d in range(1, n_row):
        peer = lax.rem(r + d, n_row)

        @pl.when(peer > r)
        def _():
            pl.semaphore_signal(barrier, inc=1, device_id={"row": peer}, device_id_type=MESH)

    def answer():
        for d in range(1, n_col):
            peer = lax.rem(c + d, n_col)

            @pl.when(lax.rem(peer, 4) * (n_col // 4) + peer // 4 < place)
            def _():
                pl.semaphore_signal(ready, inc=1, device_id={"col": peer}, device_id_type=MESH)

        for d in range(1, n_row):
            peer = lax.rem(r + d, n_row)

            @pl.when(peer < r)
            def _():
                pl.semaphore_signal(ready, inc=1, device_id={"row": peer}, device_id_type=MESH)

    def at(h, k):
        return pl.ds(h * half + k * step, step)

    def bulk(phase, d, k):
        if phase == PA:
            src, dst = s_opp.at[at(d, k)], r_opp.at[at(d, k)]
        elif phase in (PB, PC):
            h = d if phase == PC else 1 - d
            src, dst = ((s_right, r_left), (s_left, r_right))[d]
            src, dst = src.at[at(h, k)], dst.at[at(h, k)]
        else:
            h = 1 - d if phase == PX else d
            q = y if phase != PE else (left, right)[d]
            src = dst = full.at[q, at(h, k)]
        return pltpu.make_async_remote_copy(
            src_ref=src, dst_ref=dst, send_sem=send_sem.at[phase, d, k], recv_sem=recv_sem.at[phase, d, k],
            device_id={"dp": (right, left)[d]}, device_id_type=MESH)

    def arrive(phase, d, k):
        if phase < PD:
            bulk(phase, d, k).wait_recv()
            return
        h = 1 - d if phase == PX else d
        q = (left, right)[d] if phase != PE else opp
        ref = full.at[q, at(h, k)]
        pltpu.make_async_remote_copy(
            src_ref=ref, dst_ref=ref, send_sem=send_sem.at[phase, d, k], recv_sem=recv_sem.at[phase, d, k],
            device_id={"dp": (right, left)[d]}, device_id_type=MESH).wait_recv()

    loads[2].wait()
    for k in range(CHUNKS):
        for d in range(2):
            s_opp[at(d, k)] = own[2, at(d, k)].astype(f32)
    pl.semaphore_wait(barrier, n_dp - 1 + place + r)
    for k in range(CHUNKS):
        for d in range(2):
            bulk(PA, d, k).start()
    for i in (1, 3, 0, 4, 5, 6, 7, 8, 9):
        loads[i].start()
    loads[1].wait()
    loads[3].wait()
    for k in range(CHUNKS):
        for d, (dst, slot) in enumerate(((s_right, 1), (s_left, 3))):
            dst[at(1 - d, k)] = own[slot, at(1 - d, k)].astype(f32)
    answer()

    def first(k):
        for d in range(2):
            bulk(PA, d, k).wait_send()
            bulk(PB, d, k).start()

    def second(k):
        for d, (dst, slot) in enumerate(((s_right, 1), (s_left, 3))):
            arrive(PA, d, k)
            dst[at(d, k)] = r_opp[at(d, k)] + own[slot, at(d, k)].astype(f32)
            bulk(PC, d, k).start()

    first(0)
    first(1)
    for k in range(2, CHUNKS):
        second(k - 2)
        first(k)
    second(CHUNKS - 2)
    second(CHUNKS - 1)
    for q in range(4):
        loads[4 + q].wait()

    def weight_step(i, acc):
        w = held[y, pl.ds(pl.multiple_of(i * 8, 8), 8)]
        sq = w * w
        for j in range(width // 128):
            acc = acc + sq[:, j * 128:(j + 1) * 128]
        return acc

    w_lanes = lax.fori_loop(0, rows // 8, weight_step, jnp.zeros((8, 128), f32))
    loads[0].wait()
    col_acc = jnp.zeros((8, width), f32)
    for k in range(CHUNKS):
        for d in range(2):
            arrive(PB, 1 - d, k)
            arrive(PC, d, k)
            g = own[0, at(d, k)].astype(f32) + r_left[at(d, k)] + r_right[at(d, k)]
            full[y, at(d, k)] = g
            bulk(PD, d, k).start()
            sq = g * g
            for i in range(step // 8):
                col_acc = col_acc + sq[i * 8:(i + 1) * 8]
            part = sq[:, :128]
            for j in range(1, width // 128):
                part = part + sq[:, j * 128:(j + 1) * 128]
            lanes[at(d, k)] = part

    def send_small(stage, group, parts):
        mine = parts.at[group[1]]
        copies = []
        for dev in peers(group):
            copies.append(pltpu.make_async_remote_copy(
                src_ref=mine, dst_ref=mine, send_sem=xs_sem.at[stage], recv_sem=xr_sem.at[stage],
                device_id=dev, device_id_type=MESH))
            copies[-1].start()

    def all_but_one(stage, group, parts):
        rest = parts.at[pl.ds(0, group[2] - 1)]
        return pltpu.make_async_remote_copy(
            src_ref=rest, dst_ref=rest, send_sem=xs_sem.at[stage], recv_sem=xr_sem.at[stage],
            device_id=peers(group)[0], device_id_type=MESH)

    def total(parts):
        out = parts[0]
        for i in range(1, parts.shape[0]):
            out = out + parts[i]
        return out

    def others(ks):
        for k in ks:
            for d in range(2):
                bulk(PX, d, k).start()

    def forward(ks):
        for k in ks:
            for d in range(2):
                arrive(PD, d, k)
                bulk(PE, d, k).start()

    others(range(CHUNKS // 2))
    later = n_col - 1 - place + n_row - 1 - r

    @pl.when(later > 0)
    def _():
        pl.semaphore_wait(ready, later)

    col_parts[r] = jnp.sum(col_acc, axis=0, keepdims=True)
    send_small(0, row_group, col_parts)
    row_sums = jnp.sum(lanes[...].T, axis=0, keepdims=True)
    weight_sums = jnp.sum(w_lanes, axis=0, keepdims=True)
    loads[9].wait()
    col_old[...] = colm[...].reshape(col_old.shape)
    span = pl.ds(pl.multiple_of(y * width, 128), width)
    old = col_old[:, span]
    all_but_one(0, row_group, col_parts).wait_recv()
    col_mine = decay_rate * old + (1.0 - decay_rate) * (total(col_parts) / rows_all + eps_one)
    inverse = 1.0 / col_mine

    def raw_step(k, _):
        at_k = pl.ds(pl.multiple_of(k * 8, 8), 8)
        g = full[y, at_k]
        sq = g * g * inverse
        part = sq[:, :128]
        for j in range(1, width // 128):
            part = part + sq[:, j * 128:(j + 1) * 128]
        lanes[at_k] = part
        return 0

    lax.fori_loop(0, rows // 8, raw_step, 0, unroll=4)
    raw_sums = jnp.sum(lanes[...].T, axis=0, keepdims=True)
    sums_col[c] = jnp.concatenate([row_sums, raw_sums, weight_sums, jnp.zeros((5, 128), f32)], axis=0)
    send_small(1, col_group, sums_col)
    col_all[:, span] = col_mine
    for dev in peers(dp_group):
        pltpu.make_async_remote_copy(
            src_ref=col_all.at[:, span], dst_ref=col_all.at[:, span], send_sem=xs_sem.at[4],
            recv_sem=xr_sem.at[4], device_id=dev, device_id_type=MESH).start()
    others(range(CHUNKS // 2, CHUNKS))
    loads[8].wait()
    forward(range(CHUNKS // 2))
    all_but_one(1, col_group, sums_col).wait_recv()
    sums_dp[y] = total(sums_col)
    send_small(2, dp_group, sums_dp)
    forward(range(CHUNKS // 2, CHUNKS))
    all_but_one(2, dp_group, sums_dp).wait_recv()
    tile = total(sums_dp)
    row_mine = decay_rate * rowm[...].reshape(1, rows) + (1.0 - decay_rate) * (tile[0:1] / cols_all + eps_one)
    row_new[...] = row_mine
    sums_row[r] = jnp.concatenate([tile[1:2] / row_mine, row_mine, tile[2:3], jnp.zeros((5, 128), f32)], axis=0)
    send_small(3, row_group, sums_row)
    cols_rest = col_all.at[:, pl.ds(0, 3 * width)]
    col_round = pltpu.make_async_remote_copy(
        src_ref=cols_rest, dst_ref=cols_rest, send_sem=xs_sem.at[4], recv_sem=xr_sem.at[4],
        device_id=peers(dp_group)[0], device_id_type=MESH)
    col_round.wait_recv()
    col_scale[...] = lax.rsqrt(col_all[...])
    all_but_one(3, row_group, sums_row).wait_recv()
    sums = jnp.sum(total(sums_row), axis=1, keepdims=True)
    row_mean = sums[1:2] / rows_all
    clip = jnp.maximum(1.0, jnp.sqrt(sums[0:1] * row_mean / entries) / clip_level)
    size = learn_rate * jnp.maximum(eps_two, jnp.sqrt(sums[2:3] / entries))
    scal[...] = jnp.concatenate([jnp.broadcast_to(clip, (1, 128)), jnp.broadcast_to(size, (1, 128))], axis=0)
    scale = lax.rsqrt(row_mine) * (jnp.sqrt(row_mean) / clip)
    row_scale[...] = jnp.broadcast_to(scale, (128, 128)).T
    for k in range(CHUNKS):
        for d in range(2):
            arrive(PX, d, k)
            arrive(PE, d, k)
    for stage, (group, parts) in enumerate(
            ((row_group, col_parts), (col_group, sums_col), (dp_group, sums_dp), (row_group, sums_row))):
        all_but_one(stage, group, parts).wait_send()
    col_round.wait_send()
    for phase in (PB, PC, PD, PX, PE):
        for k in range(CHUNKS):
            for d in range(2):
                bulk(phase, d, k).wait_send()


def update_kernel(full, held, col_all, row_new, row_scale, col_scale, scal,
                  weight_out, update_out, row_out, col_out, clip_out,
                  new_weight, update, sem):
    rows, width = full.shape[1], full.shape[2]
    size = scal[1:2, :]
    step = 16
    copies = []
    for k in range(rows // step):
        for i in range(step // 8):
            at = pl.ds(k * step + i * 8, 8)
            by_row = row_scale[at]
            for q in range(4):
                for j in range(width // 128):
                    col = pl.ds(j * 128, 128)
                    out = pl.ds(q * width + j * 128, 128)
                    u = full[q, at, col] * by_row * col_scale[:, out]
                    update[at, out] = u
                    new_weight[at, out] = held[q, at, col] - size * u
        at = pl.ds(k * step, step)
        for which, (src, dst) in enumerate(((update, update_out), (new_weight, weight_out))):
            copies.append(pltpu.make_async_copy(src.at[at], dst.at[at], sem.at[which, k]))
            copies[-1].start()
    row_out[...] = row_new[...].reshape(row_out.shape)
    col_out[...] = col_all[...].reshape(col_out.shape)
    clip_out[...] = scal[0:1, 0:1]
    for copy in copies:
        copy.wait()


def solution(mesh):
    n_dp, n_row, n_col = mesh.shape["dp"], mesh.shape["row"], mesh.shape["col"]
    sizes = (n_dp, n_row, n_col)

    def body(weight, grad_parts, row_moment, col_moment):
        rows, cols = weight.shape
        width = cols // n_dp
        vmem = pl.BlockSpec(memory_space=pltpu.VMEM)
        hbm = pl.BlockSpec(memory_space=pltpu.HBM)
        shapes = ((4, rows, width), (4, rows, width), (1, cols), (1, rows), (rows, 128), (1, cols), (2, 128))
        outs = pl.pallas_call(
            functools.partial(exchange_kernel, sizes),
            out_shape=tuple(pltpu.VMEM(s, f32) for s in shapes),
            in_specs=[hbm] * 4,
            out_specs=(vmem,) * len(shapes),
            scratch_shapes=[
                pltpu.VMEM((4, rows, width), jnp.bfloat16),
                *[pltpu.VMEM((rows, width), f32) for _ in range(6)],
                pltpu.VMEM((rows, 128), f32),
                pltpu.VMEM((rows,), f32),
                pltpu.VMEM((cols,), f32),
                pltpu.VMEM((1, cols), f32),
                pltpu.VMEM((n_row, 1, width), f32),
                pltpu.VMEM((n_col, 8, 128), f32),
                pltpu.VMEM((n_dp, 8, 128), f32),
                pltpu.VMEM((n_row, 8, 128), f32),
                pltpu.SemaphoreType.DMA((10,)),
                pltpu.SemaphoreType.DMA((6, 2, CHUNKS)),
                pltpu.SemaphoreType.DMA((6, 2, CHUNKS)),
                pltpu.SemaphoreType.DMA((5,)),
                pltpu.SemaphoreType.DMA((5,)),
                pltpu.SemaphoreType.REGULAR,
            ],
            compiler_params=pltpu.CompilerParams(
                collective_id=0, has_side_effects=True, vmem_limit_bytes=24 << 20),
            name="exchange",
        )(*(pltpu.with_memory_space_constraint(a, pltpu.HBM) for a in (grad_parts, weight, row_moment, col_moment)))
        new_weight, update, row_new, col_new, clip = pl.pallas_call(
            update_kernel,
            out_shape=(
                jax.ShapeDtypeStruct((rows, cols), f32),
                jax.ShapeDtypeStruct((rows, cols), f32),
                jax.ShapeDtypeStruct((rows,), f32),
                jax.ShapeDtypeStruct((cols,), f32),
                jax.ShapeDtypeStruct((1, 1), f32),
            ),
            in_specs=[vmem] * len(shapes),
            out_specs=(pl.BlockSpec(memory_space=pl.ANY), pl.BlockSpec(memory_space=pl.ANY), vmem, vmem, vmem),
            scratch_shapes=[
                pltpu.VMEM((rows, cols), f32),
                pltpu.VMEM((rows, cols), f32),
                pltpu.SemaphoreType.DMA((2, rows // 16)),
            ],
            compiler_params=pltpu.CompilerParams(vmem_limit_bytes=24 << 20),
            name="apply",
        )(*outs)
        return new_weight, update, row_new, col_new, clip.reshape(())

    return jax.shard_map(
        body,
        mesh=mesh,
        in_specs=(P("row", "col"), P("dp", "row", "col"), P("row"), P("col")),
        out_specs=(P("row", "col"), P("row", "col"), P("row"), P("col"), P()),
        check_vma=False,
    )
```

```python
import functools

import jax
import jax.numpy as jnp
from jax import lax
from jax.experimental import pallas as pl
from jax.experimental.pallas import tpu as pltpu
from jax.sharding import PartitionSpec as P

decay_rate = 0.5
eps_one = 1e-30
eps_two = 0.001
learn_rate = 0.01
clip_level = 1.0

MESH = pl.DeviceIdType.MESH
f32 = jnp.float32
PA, PB, PC, PD, PX, PE = range(6)
PIECES = (4, 1, 4, 4, 1, 4)


def exchange_kernel(sizes, grad_hbm, weight_hbm, rowm_hbm, colm_hbm,
                    full, held, col_all, row_new, row_scale, col_scale, scal,
                    own, s_opp, s_right, s_left, r_opp, r_left, r_right, lanes,
                    rowm, colm, col_old, col_parts, sums_yx, sums_zr,
                    load_sem, send_sem, recv_sem, xs_sem, xr_sem, ready):
    rows_all, cols_all = sizes
    rows, width = own.shape[1], own.shape[2]
    half = rows // 2
    entries = float(rows_all) * float(cols_all)
    y, r, c = lax.axis_index("dp"), lax.axis_index("row"), lax.axis_index("col")
    x, z = c // 4, lax.rem(c, 4)
    right, opp, left = lax.rem(y + 1, 4), lax.rem(y + 2, 4), lax.rem(y + 3, 4)

    loads = {}
    for slot, q in ((2, opp), (1, right), (3, left), (0, y)):
        loads[slot] = pltpu.make_async_copy(
            grad_hbm.at[0, :, pl.ds(pl.multiple_of(q * width, 128), width)], own.at[slot], load_sem.at[slot])
    for q in range(4):
        loads[4 + q] = pltpu.make_async_copy(
            weight_hbm.at[:, pl.ds(q * width, width)], held.at[q], load_sem.at[4 + q])
    loads[8] = pltpu.make_async_copy(rowm_hbm, rowm, load_sem.at[8])
    loads[9] = pltpu.make_async_copy(colm_hbm, colm, load_sem.at[9])

    barrier = pltpu.get_barrier_semaphore()
    place = z * 4 + r

    def greet(sem, later):
        sign = 1 if later else -1
        for d in range(1, 4):
            for which, at in (("x", x), ("z", z), ("r", r)):
                to = at + sign * d

                @pl.when((to < 4) if later else (to >= 0))
                def _():
                    for i in range(4):
                        if which == "x":
                            dev = {"dp": i, "col": to * 4 + z}
                        elif which == "z":
                            dev = {"col": x * 4 + to, "row": i}
                        else:
                            dev = {"row": to}
                        if which != "r" or i == 0:
                            pl.semaphore_signal(sem, inc=1, device_id=dev, device_id_type=MESH)

    for q in (right, left, opp):
        pl.semaphore_signal(barrier, inc=1, device_id={"dp": q}, device_id_type=MESH)
    loads[2].start()
    greet(barrier, True)

    def at(phase, h, k):
        step = half // PIECES[phase]
        return pl.ds(h * half + k * step, step)

    def bulk(phase, d, k=0):
        if phase == PA:
            src, dst = s_opp.at[at(phase, d, k)], r_opp.at[at(phase, d, k)]
        elif phase in (PB, PC):
            h = d if phase == PC else 1 - d
            src, dst = ((s_right, r_left), (s_left, r_right))[d]
            src, dst = src.at[at(phase, h, k)], dst.at[at(phase, h, k)]
        else:
            h = 1 - d if phase == PX else d
            q = y if phase != PE else (left, right)[d]
            src = dst = full.at[q, at(phase, h, k)]
        return pltpu.make_async_remote_copy(
            src_ref=src, dst_ref=dst, send_sem=send_sem.at[phase, d, k], recv_sem=recv_sem.at[phase, d, k],
            device_id={"dp": (right, left)[d]}, device_id_type=MESH)

    def arrive(phase, d, k=0):
        if phase < PD:
            bulk(phase, d, k).wait_recv()
            return
        h = 1 - d if phase == PX else d
        q = (left, right)[d] if phase != PE else opp
        ref = full.at[q, at(phase, h, k)]
        pltpu.make_async_remote_copy(
            src_ref=ref, dst_ref=ref, send_sem=send_sem.at[phase, d, k], recv_sem=recv_sem.at[phase, d, k],
            device_id={"dp": (right, left)[d]}, device_id_type=MESH).wait_recv()

    def sent(phase):
        for k in range(PIECES[phase]):
            for d in range(2):
                bulk(phase, d, k).wait_send()

    loads[2].wait()
    s_opp[...] = own[2].astype(f32)
    pl.semaphore_wait(barrier, 3 + 4 * x + place)
    for k in range(PIECES[PA]):
        for d in range(2):
            bulk(PA, d, k).start()
    for i in (1, 3, 0, 4, 5, 6, 7, 8, 9):
        loads[i].start()
    loads[1].wait()
    loads[3].wait()
    for d, (dst, slot) in enumerate(((s_right, 1), (s_left, 3))):
        span = at(PB, 1 - d, 0)
        dst[span] = own[slot, span].astype(f32)
        bulk(PB, d).start()
    greet(ready, False)
    for i in (0, 4, 5, 6, 7, 8, 9):
        loads[i].wait()

    def weight_step(i, acc):
        w = held[y, pl.ds(pl.multiple_of(i * 8, 8), 8)]
        sq = w * w
        for j in range(width // 128):
            acc = acc + sq[:, j * 128:(j + 1) * 128]
        return acc

    w_lanes = lax.fori_loop(0, rows // 8, weight_step, jnp.zeros((8, 128), f32), unroll=2)
    weight_sums = jnp.sum(w_lanes, axis=0, keepdims=True)
    col_old[...] = colm[...].reshape(col_old.shape)
    mine = pl.ds(pl.multiple_of(y * width, 128), width)
    row_old = rowm[...].reshape(1, rows)
    for k in range(PIECES[PC]):
        for d, (dst, slot) in enumerate(((s_right, 1), (s_left, 3))):
            span = at(PC, d, k)
            arrive(PA, d, k)
            dst[span] = r_opp[span] + own[slot, span].astype(f32)
            bulk(PC, d, k).start()
    sent(PA)
    col_acc = jnp.zeros((8, width), f32)
    arrive(PB, 0)
    arrive(PB, 1)
    for k in range(PIECES[PC]):
        for d in range(2):
            span = at(PC, d, k)
            arrive(PC, d, k)
            g = own[0, span].astype(f32) + r_left[span] + r_right[span]
            full[y, span] = g
            bulk(PD, d, k).start()
            sq = g * g
            for i in range(sq.shape[0] // 8):
                col_acc = col_acc + sq[i * 8:(i + 1) * 8]
            part = sq[:, :128]
            for j in range(1, width // 128):
                part = part + sq[:, j * 128:(j + 1) * 128]
            lanes[span] = part

    def send_small(stage, parts, at, devs):
        ref = parts.at[at]
        for i, dev in devs:
            @pl.when(at != i)
            def _():
                pltpu.make_async_remote_copy(
                    src_ref=ref, dst_ref=ref, send_sem=xs_sem.at[stage], recv_sem=xr_sem.at[stage],
                    device_id=dev, device_id_type=MESH).start()

    def whole(stage, parts, dev):
        rest = parts.at[pl.ds(0, parts.shape[0] - 1)]
        return pltpu.make_async_remote_copy(
            src_ref=rest, dst_ref=rest, send_sem=xs_sem.at[stage], recv_sem=xr_sem.at[stage],
            device_id=dev, device_id_type=MESH)

    def total(parts):
        out = parts[0]
        for i in range(1, parts.shape[0]):
            out = out + parts[i]
        return out

    near = {"row": lax.rem(r + 1, 4)}
    later = 12 - 4 * x + 15 - place

    @pl.when(later > 0)
    def _():
        pl.semaphore_wait(ready, later)

    col_parts[r] = jnp.sum(col_acc, axis=0, keepdims=True)
    send_small(0, col_parts, r, [(i, {"row": i}) for i in range(4)])
    row_sums = jnp.sum(lanes[...].T, axis=0, keepdims=True)
    old = decay_rate * col_old[:, mine]
    whole(0, col_parts, near).wait_recv()
    col_mine = old + (1.0 - decay_rate) * (total(col_parts) / rows_all + eps_one)
    inverse = 1.0 / col_mine

    def raw_step(k, _):
        span = pl.ds(pl.multiple_of(k * 8, 8), 8)
        g = full[y, span]
        sq = g * g * inverse
        part = sq[:, :128]
        for j in range(1, width // 128):
            part = part + sq[:, j * 128:(j + 1) * 128]
        lanes[span] = part
        return 0

    lax.fori_loop(0, rows // 8, raw_step, 0, unroll=4)
    raw_sums = jnp.sum(lanes[...].T, axis=0, keepdims=True)
    sums_yx[y * 4 + x] = jnp.concatenate([row_sums, raw_sums, weight_sums, jnp.zeros((5, 128), f32)], axis=0)
    send_small(1, sums_yx, y * 4 + x, [(i * 4 + j, {"dp": i, "col": j * 4 + z}) for i in range(4) for j in range(4)])
    for d in range(2):
        bulk(PX, d).start()
    col_all[:, mine] = col_mine
    for q in (right, left, opp):
        pltpu.make_async_remote_copy(
            src_ref=col_all.at[:, mine], dst_ref=col_all.at[:, mine], send_sem=xs_sem.at[3],
            recv_sem=xr_sem.at[3], device_id={"dp": q}, device_id_type=MESH).start()
    for k in range(PIECES[PE]):
        for d in range(2):
            arrive(PD, d, k)
            bulk(PE, d, k).start()
    whole(1, sums_yx, {"dp": right}).wait_recv()
    sums_zr[place] = jnp.concatenate([total(sums_yx)[0:3], row_old, jnp.zeros((4, 128), f32)], axis=0)
    send_small(2, sums_zr, place, [(i * 4 + j, {"col": x * 4 + i, "row": j}) for i in range(4) for j in range(4)])
    cols_rest = col_all.at[:, pl.ds(0, 3 * width)]
    cols = pltpu.make_async_remote_copy(
        src_ref=cols_rest, dst_ref=cols_rest, send_sem=xs_sem.at[3], recv_sem=xr_sem.at[3],
        device_id={"dp": right}, device_id_type=MESH)
    cols.wait()
    col_scale[...] = lax.rsqrt(col_all[...])
    whole(0, col_parts, near).wait_send()
    whole(1, sums_yx, {"dp": right}).wait_send()
    for phase in (PB, PC, PD, PX, PE):
        sent(phase)
    for d in range(2):
        arrive(PX, d)
        for k in range(PIECES[PE]):
            arrive(PE, d, k)
    whole(2, sums_zr, near).wait_recv()

    def moments(group):
        tile = sums_zr[group]
        for i in range(1, 4):
            tile = tile + sums_zr[i * 4 + group]
        return tile, (decay_rate * 0.25) * tile[3:4] + (1.0 - decay_rate) * (tile[0:1] / cols_all + eps_one)

    _, row_mine = moments(r)
    row_new[...] = row_mine
    row_scale[...] = jnp.broadcast_to(lax.rsqrt(row_mine), (128, 128)).T
    sums = [jnp.zeros((1, 128), f32)] * 3
    for group in range(4):
        tile, row_one = moments(group)
        for i, part in enumerate((tile[1:2] / row_one, row_one, tile[2:3])):
            sums[i] = sums[i] + part
    sums = jnp.sum(jnp.concatenate(sums, axis=0), axis=1, keepdims=True)
    row_mean = sums[1:2] / rows_all
    clip = jnp.maximum(1.0, jnp.sqrt(sums[0:1] * row_mean / entries) / clip_level)
    size = learn_rate * jnp.maximum(eps_two, jnp.sqrt(sums[2:3] / entries))
    scal[...] = jnp.concatenate(
        [jnp.broadcast_to(v, (1, 128)) for v in (clip, size, jnp.sqrt(row_mean) / clip, clip)], axis=0)
    whole(2, sums_zr, near).wait_send()


def update_kernel(full, held, col_all, row_new, row_scale, col_scale, scal,
                  weight_out, update_out, row_out, col_out, clip_out,
                  new_weight, update, sem):
    rows, width = full.shape[1], full.shape[2]
    size, factor = scal[1:2, :], scal[2:3, :]
    step = 16
    copies = []
    for k in range(rows // step):
        for i in range(step // 8):
            at = pl.ds(k * step + i * 8, 8)
            by_row = row_scale[at] * factor
            for q in range(4):
                for j in range(width // 128):
                    col = pl.ds(j * 128, 128)
                    out = pl.ds(q * width + j * 128, 128)
                    u = full[q, at, col] * by_row * col_scale[:, out]
                    update[at, out] = u
                    new_weight[at, out] = held[q, at, col] - size * u
        at = pl.ds(k * step, step)
        for which, (src, dst) in enumerate(((update, update_out), (new_weight, weight_out))):
            copies.append(pltpu.make_async_copy(src.at[at], dst.at[at], sem.at[which, k]))
            copies[-1].start()
    row_out[...] = row_new[...].reshape(row_out.shape)
    col_out[...] = col_all[...].reshape(col_out.shape)
    clip_out[...] = scal[0:1, 0:1]
    for copy in copies:
        copy.wait()


def solution(mesh):
    assert all(mesh.shape[axis] == size for axis, size in (("dp", 4), ("row", 4), ("col", 16)))

    def body(weight, grad_parts, row_moment, col_moment):
        rows, cols = weight.shape
        width = cols // 4
        vmem = pl.BlockSpec(memory_space=pltpu.VMEM)
        hbm = pl.BlockSpec(memory_space=pltpu.HBM)
        shapes = ((4, rows, width), (4, rows, width), (1, cols), (1, rows), (rows, 128), (1, cols), (4, 128))
        outs = pl.pallas_call(
            functools.partial(exchange_kernel, (rows * 4, cols * 16)),
            out_shape=tuple(pltpu.VMEM(s, f32) for s in shapes),
            in_specs=[hbm] * 4,
            out_specs=(vmem,) * len(shapes),
            scratch_shapes=[
                pltpu.VMEM((4, rows, width), jnp.bfloat16),
                *[pltpu.VMEM((rows, width), f32) for _ in range(6)],
                pltpu.VMEM((rows, 128), f32),
                pltpu.VMEM((rows,), f32),
                pltpu.VMEM((cols,), f32),
                pltpu.VMEM((1, cols), f32),
                pltpu.VMEM((4, 1, width), f32),
                pltpu.VMEM((16, 8, 128), f32),
                pltpu.VMEM((16, 8, 128), f32),
                pltpu.SemaphoreType.DMA((10,)),
                pltpu.SemaphoreType.DMA((6, 2, max(PIECES))),
                pltpu.SemaphoreType.DMA((6, 2, max(PIECES))),
                pltpu.SemaphoreType.DMA((4,)),
                pltpu.SemaphoreType.DMA((4,)),
                pltpu.SemaphoreType.REGULAR,
            ],
            compiler_params=pltpu.CompilerParams(
                collective_id=0, has_side_effects=True, vmem_limit_bytes=24 << 20),
            name="exchange",
        )(*(pltpu.with_memory_space_constraint(a, pltpu.HBM) for a in (grad_parts, weight, row_moment, col_moment)))
        new_weight, update, row_new, col_new, clip = pl.pallas_call(
            update_kernel,
            out_shape=(
                jax.ShapeDtypeStruct((rows, cols), f32),
                jax.ShapeDtypeStruct((rows, cols), f32),
                jax.ShapeDtypeStruct((rows,), f32),
                jax.ShapeDtypeStruct((cols,), f32),
                jax.ShapeDtypeStruct((1, 1), f32),
            ),
            in_specs=[vmem] * len(shapes),
            out_specs=(pl.BlockSpec(memory_space=pl.ANY), pl.BlockSpec(memory_space=pl.ANY), vmem, vmem, vmem),
            scratch_shapes=[
                pltpu.VMEM((rows, cols), f32),
                pltpu.VMEM((rows, cols), f32),
                pltpu.SemaphoreType.DMA((2, rows // 16)),
            ],
            compiler_params=pltpu.CompilerParams(vmem_limit_bytes=24 << 20),
            name="apply",
        )(*outs)
        return new_weight, update, row_new, col_new, clip.reshape(())

    return jax.shard_map(
        body,
        mesh=mesh,
        in_specs=(P("row", "col"), P("dp", "row", "col"), P("row"), P("col")),
        out_specs=(P("row", "col"), P("row", "col"), P("row"), P("col"), P()),
        check_vma=False,
    )
```

```python
import functools

import jax
import jax.numpy as jnp
from jax import lax
from jax.experimental import pallas as pl
from jax.experimental.pallas import tpu as pltpu
from jax.sharding import PartitionSpec as P

decay_rate = 0.5
eps_one = 1e-30
eps_two = 0.001
learn_rate = 0.01
clip_level = 1.0

MESH = pl.DeviceIdType.MESH
f32 = jnp.float32
PA, PB, PC, PD, PX, PE = range(6)
PIECES = (4, 1, 4, 4, 4, 4)


def exchange_kernel(sizes, grad_hbm, weight_hbm, rowm_hbm, colm_hbm,
                    full, held, col_all, row_new, row_scale, col_scale, scal,
                    own, s_opp, s_right, s_left, r_opp, r_left, r_right, lanes,
                    rowm, colm, col_old, col_parts, sums_yx, sums_zr,
                    load_sem, send_sem, recv_sem, xs_sem, xr_sem, ready):
    rows_all, cols_all = sizes
    rows, width = own.shape[1], own.shape[2]
    half = rows // 2
    entries = float(rows_all) * float(cols_all)
    y, r, c = lax.axis_index("dp"), lax.axis_index("row"), lax.axis_index("col")
    x, z = c // 4, lax.rem(c, 4)
    right, opp, left = lax.rem(y + 1, 4), lax.rem(y + 2, 4), lax.rem(y + 3, 4)

    loads = {}
    for slot, q in ((2, opp), (1, right), (3, left), (0, y)):
        loads[slot] = pltpu.make_async_copy(
            grad_hbm.at[0, :, pl.ds(pl.multiple_of(q * width, 128), width)], own.at[slot], load_sem.at[slot])
    for q in range(4):
        loads[4 + q] = pltpu.make_async_copy(
            weight_hbm.at[:, pl.ds(q * width, width)], held.at[q], load_sem.at[4 + q])
    loads[8] = pltpu.make_async_copy(rowm_hbm, rowm, load_sem.at[8])
    loads[9] = pltpu.make_async_copy(colm_hbm, colm, load_sem.at[9])

    barrier = pltpu.get_barrier_semaphore()
    place = z * 4 + r

    def greet(sem, later):
        sign = 1 if later else -1
        for d in range(1, 4):
            for which, at in (("x", x), ("z", z), ("r", r)):
                to = at + sign * d

                @pl.when((to < 4) if later else (to >= 0))
                def _():
                    for i in range(4):
                        if which == "x":
                            dev = {"dp": i, "col": to * 4 + z}
                        elif which == "z":
                            dev = {"col": x * 4 + to, "row": i}
                        else:
                            dev = {"row": to}
                        if which != "r" or i == 0:
                            pl.semaphore_signal(sem, inc=1, device_id=dev, device_id_type=MESH)

    loads[2].start()
    for q in (right, left, opp):
        pl.semaphore_signal(barrier, inc=1, device_id={"dp": q}, device_id_type=MESH)
    greet(barrier, True)

    def at(phase, h, k):
        step = half // PIECES[phase]
        return pl.ds(h * half + k * step, step)

    def bulk(phase, d, k=0):
        if phase == PA:
            src, dst = s_opp.at[at(phase, d, k)], r_opp.at[at(phase, d, k)]
        elif phase in (PB, PC):
            h = d if phase == PC else 1 - d
            src, dst = ((s_right, r_left), (s_left, r_right))[d]
            src, dst = src.at[at(phase, h, k)], dst.at[at(phase, h, k)]
        else:
            h = 1 - d if phase == PX else d
            q = y if phase != PE else (left, right)[d]
            src = dst = full.at[q, at(phase, h, k)]
        return pltpu.make_async_remote_copy(
            src_ref=src, dst_ref=dst, send_sem=send_sem.at[phase, d, k], recv_sem=recv_sem.at[phase, d, k],
            device_id={"dp": (right, left)[d]}, device_id_type=MESH)

    def arrive(phase, d, k=0):
        if phase < PD:
            bulk(phase, d, k).wait_recv()
            return
        h = 1 - d if phase == PX else d
        q = (left, right)[d] if phase != PE else opp
        ref = full.at[q, at(phase, h, k)]
        pltpu.make_async_remote_copy(
            src_ref=ref, dst_ref=ref, send_sem=send_sem.at[phase, d, k], recv_sem=recv_sem.at[phase, d, k],
            device_id={"dp": (right, left)[d]}, device_id_type=MESH).wait_recv()

    def sent(phase):
        for k in range(PIECES[phase]):
            for d in range(2):
                bulk(phase, d, k).wait_send()

    loads[2].wait()
    for k in range(PIECES[PA]):
        for d in range(2):
            span = at(PA, d, k)
            s_opp[span] = own[2, span].astype(f32)
        if k == 0:
            pl.semaphore_wait(barrier, 3 + 4 * x + place)
        for d in range(2):
            bulk(PA, d, k).start()
    for i in (1, 3, 0, 4, 5, 6, 7, 8, 9):
        loads[i].start()
    loads[1].wait()
    loads[3].wait()
    for d, (dst, slot) in enumerate(((s_right, 1), (s_left, 3))):
        span = at(PB, 1 - d, 0)
        dst[span] = own[slot, span].astype(f32)
        bulk(PB, d).start()
    greet(ready, False)
    for i in (0, 4, 5, 6, 7, 8, 9):
        loads[i].wait()

    def weight_step(i, acc):
        w = held[y, pl.ds(pl.multiple_of(i * 8, 8), 8)]
        sq = w * w
        for j in range(width // 128):
            acc = acc + sq[:, j * 128:(j + 1) * 128]
        return acc

    w_lanes = lax.fori_loop(0, rows // 8, weight_step, jnp.zeros((8, 128), f32), unroll=2)
    weight_sums = jnp.sum(w_lanes, axis=0, keepdims=True)
    col_old[...] = colm[...].reshape(col_old.shape)
    mine = pl.ds(pl.multiple_of(y * width, 128), width)
    row_old = rowm[...].reshape(1, rows)
    for k in range(PIECES[PC]):
        for d, (dst, slot) in enumerate(((s_right, 1), (s_left, 3))):
            span = at(PC, d, k)
            arrive(PA, d, k)
            dst[span] = r_opp[span] + own[slot, span].astype(f32)
            bulk(PC, d, k).start()
    sent(PA)
    col_acc = jnp.zeros((8, width), f32)
    arrive(PB, 0)
    arrive(PB, 1)
    for k in range(PIECES[PC]):
        for d in range(2):
            span = at(PC, d, k)
            arrive(PC, d, k)
            g = own[0, span].astype(f32) + r_left[span] + r_right[span]
            full[y, span] = g
            bulk(PD, d, k).start()
            sq = g * g
            for i in range(sq.shape[0] // 8):
                col_acc = col_acc + sq[i * 8:(i + 1) * 8]
            part = sq[:, :128]
            for j in range(1, width // 128):
                part = part + sq[:, j * 128:(j + 1) * 128]
            lanes[span] = part

    def send_small(stage, parts, at, devs):
        ref = parts.at[at]
        for i, dev in devs:
            @pl.when(at != i)
            def _():
                pltpu.make_async_remote_copy(
                    src_ref=ref, dst_ref=ref, send_sem=xs_sem.at[stage], recv_sem=xr_sem.at[stage],
                    device_id=dev, device_id_type=MESH).start()

    def whole(stage, parts, dev):
        rest = parts.at[pl.ds(0, parts.shape[0] - 1)]
        return pltpu.make_async_remote_copy(
            src_ref=rest, dst_ref=rest, send_sem=xs_sem.at[stage], recv_sem=xr_sem.at[stage],
            device_id=dev, device_id_type=MESH)

    def total(parts):
        out = parts[0]
        for i in range(1, parts.shape[0]):
            out = out + parts[i]
        return out

    near = {"row": lax.rem(r + 1, 4)}
    later = 12 - 4 * x + 15 - place

    @pl.when(later > 0)
    def _():
        pl.semaphore_wait(ready, later)

    def others(first, last):
        for k in range(first, last):
            for d in range(2):
                bulk(PX, d, k).start()

    col_parts[r] = jnp.sum(col_acc, axis=0, keepdims=True)
    send_small(0, col_parts, r, [(i, {"row": i}) for i in range(4)])
    others(0, 1)
    row_sums = jnp.sum(lanes[...].T, axis=0, keepdims=True)
    old = decay_rate * col_old[:, mine]
    whole(0, col_parts, near).wait_recv()
    col_mine = old + (1.0 - decay_rate) * (total(col_parts) / rows_all + eps_one)
    inverse = 1.0 / col_mine

    def raw_step(k, _):
        span = pl.ds(pl.multiple_of(k * 8, 8), 8)
        g = full[y, span]
        sq = g * g * inverse
        part = sq[:, :128]
        for j in range(1, width // 128):
            part = part + sq[:, j * 128:(j + 1) * 128]
        lanes[span] = part
        return 0

    lax.fori_loop(0, rows // 8, raw_step, 0, unroll=4)
    raw_sums = jnp.sum(lanes[...].T, axis=0, keepdims=True)
    sums_yx[y * 4 + x] = jnp.concatenate([row_sums, raw_sums, weight_sums, jnp.zeros((5, 128), f32)], axis=0)
    send_small(1, sums_yx, y * 4 + x, [(i * 4 + j, {"dp": i, "col": j * 4 + z}) for i in range(4) for j in range(4)])
    others(1, PIECES[PX])
    col_all[:, mine] = col_mine
    for q in (right, left, opp):
        pltpu.make_async_remote_copy(
            src_ref=col_all.at[:, mine], dst_ref=col_all.at[:, mine], send_sem=xs_sem.at[3],
            recv_sem=xr_sem.at[3], device_id={"dp": q}, device_id_type=MESH).start()
    for k in range(PIECES[PE]):
        for d in range(2):
            arrive(PD, d, k)
            bulk(PE, d, k).start()
    whole(1, sums_yx, {"dp": right}).wait_recv()
    sums_zr[place] = jnp.concatenate([total(sums_yx)[0:3], row_old, jnp.zeros((4, 128), f32)], axis=0)
    send_small(2, sums_zr, place, [(i * 4 + j, {"col": x * 4 + i, "row": j}) for i in range(4) for j in range(4)])
    cols_rest = col_all.at[:, pl.ds(0, 3 * width)]
    cols = pltpu.make_async_remote_copy(
        src_ref=cols_rest, dst_ref=cols_rest, send_sem=xs_sem.at[3], recv_sem=xr_sem.at[3],
        device_id={"dp": right}, device_id_type=MESH)
    cols.wait()
    col_scale[...] = lax.rsqrt(col_all[...])
    whole(0, col_parts, near).wait_send()
    whole(1, sums_yx, {"dp": right}).wait_send()
    for phase in (PB, PC, PD, PX):
        sent(phase)
    for k in range(PIECES[PX]):
        for d in range(2):
            arrive(PX, d, k)
    last = PIECES[PE] - 1
    for k in range(last):
        for d in range(2):
            bulk(PE, d, k).wait_send()
            arrive(PE, d, k)
    whole(2, sums_zr, near).wait_recv()

    def moments(group):
        tile = sums_zr[group]
        for i in range(1, 4):
            tile = tile + sums_zr[i * 4 + group]
        return tile, (decay_rate * 0.25) * tile[3:4] + (1.0 - decay_rate) * (tile[0:1] / cols_all + eps_one)

    _, row_mine = moments(r)
    row_new[...] = row_mine
    row_scale[...] = jnp.broadcast_to(lax.rsqrt(row_mine), (128, 128)).T
    sums = [jnp.zeros((1, 128), f32)] * 3
    for group in range(4):
        tile, row_one = moments(group)
        for i, part in enumerate((tile[1:2] / row_one, row_one, tile[2:3])):
            sums[i] = sums[i] + part
    sums = jnp.sum(jnp.concatenate(sums, axis=0), axis=1, keepdims=True)
    row_mean = sums[1:2] / rows_all
    clip = jnp.maximum(1.0, jnp.sqrt(sums[0:1] * row_mean / entries) / clip_level)
    size = learn_rate * jnp.maximum(eps_two, jnp.sqrt(sums[2:3] / entries))
    scal[...] = jnp.concatenate(
        [jnp.broadcast_to(v, (1, 128)) for v in (clip, size, jnp.sqrt(row_mean) / clip, clip)], axis=0)
    for d in range(2):
        bulk(PE, d, last).wait_send()
        arrive(PE, d, last)
    whole(2, sums_zr, near).wait_send()


def update_kernel(full, held, col_all, row_new, row_scale, col_scale, scal,
                  weight_out, update_out, row_out, col_out, clip_out,
                  new_weight, update, sem):
    rows, width = full.shape[1], full.shape[2]
    size, factor = scal[1:2, :], scal[2:3, :]
    step = 16
    copies = []
    for k in range(rows // step):
        for i in range(step // 8):
            at = pl.ds(k * step + i * 8, 8)
            by_row = row_scale[at] * factor
            for q in range(4):
                for j in range(width // 128):
                    col = pl.ds(j * 128, 128)
                    out = pl.ds(q * width + j * 128, 128)
                    u = full[q, at, col] * by_row * col_scale[:, out]
                    update[at, out] = u
                    new_weight[at, out] = held[q, at, col] - size * u
        at = pl.ds(k * step, step)
        for which, (src, dst) in enumerate(((update, update_out), (new_weight, weight_out))):
            copies.append(pltpu.make_async_copy(src.at[at], dst.at[at], sem.at[which, k]))
            copies[-1].start()
    row_out[...] = row_new[...].reshape(row_out.shape)
    col_out[...] = col_all[...].reshape(col_out.shape)
    clip_out[...] = scal[0:1, 0:1]
    for copy in copies:
        copy.wait()


def solution(mesh):
    assert all(mesh.shape[axis] == size for axis, size in (("dp", 4), ("row", 4), ("col", 16)))

    def body(weight, grad_parts, row_moment, col_moment):
        rows, cols = weight.shape
        width = cols // 4
        vmem = pl.BlockSpec(memory_space=pltpu.VMEM)
        hbm = pl.BlockSpec(memory_space=pltpu.HBM)
        shapes = ((4, rows, width), (4, rows, width), (1, cols), (1, rows), (rows, 128), (1, cols), (4, 128))
        outs = pl.pallas_call(
            functools.partial(exchange_kernel, (rows * 4, cols * 16)),
            out_shape=tuple(pltpu.VMEM(s, f32) for s in shapes),
            in_specs=[hbm] * 4,
            out_specs=(vmem,) * len(shapes),
            scratch_shapes=[
                pltpu.VMEM((4, rows, width), jnp.bfloat16),
                *[pltpu.VMEM((rows, width), f32) for _ in range(6)],
                pltpu.VMEM((rows, 128), f32),
                pltpu.VMEM((rows,), f32),
                pltpu.VMEM((cols,), f32),
                pltpu.VMEM((1, cols), f32),
                pltpu.VMEM((4, 1, width), f32),
                pltpu.VMEM((16, 8, 128), f32),
                pltpu.VMEM((16, 8, 128), f32),
                pltpu.SemaphoreType.DMA((10,)),
                pltpu.SemaphoreType.DMA((6, 2, max(PIECES))),
                pltpu.SemaphoreType.DMA((6, 2, max(PIECES))),
                pltpu.SemaphoreType.DMA((4,)),
                pltpu.SemaphoreType.DMA((4,)),
                pltpu.SemaphoreType.REGULAR,
            ],
            compiler_params=pltpu.CompilerParams(
                collective_id=0, has_side_effects=True, vmem_limit_bytes=24 << 20),
            name="exchange",
        )(*(pltpu.with_memory_space_constraint(a, pltpu.HBM) for a in (grad_parts, weight, row_moment, col_moment)))
        new_weight, update, row_new, col_new, clip = pl.pallas_call(
            update_kernel,
            out_shape=(
                jax.ShapeDtypeStruct((rows, cols), f32),
                jax.ShapeDtypeStruct((rows, cols), f32),
                jax.ShapeDtypeStruct((rows,), f32),
                jax.ShapeDtypeStruct((cols,), f32),
                jax.ShapeDtypeStruct((1, 1), f32),
            ),
            in_specs=[vmem] * len(shapes),
            out_specs=(pl.BlockSpec(memory_space=pl.ANY), pl.BlockSpec(memory_space=pl.ANY), vmem, vmem, vmem),
            scratch_shapes=[
                pltpu.VMEM((rows, cols), f32),
                pltpu.VMEM((rows, cols), f32),
                pltpu.SemaphoreType.DMA((2, rows // 16)),
            ],
            compiler_params=pltpu.CompilerParams(vmem_limit_bytes=24 << 20),
            name="apply",
        )(*outs)
        return new_weight, update, row_new, col_new, clip.reshape(())

    return jax.shard_map(
        body,
        mesh=mesh,
        in_specs=(P("row", "col"), P("dp", "row", "col"), P("row"), P("col")),
        out_specs=(P("row", "col"), P("row", "col"), P("row"), P("col"), P()),
        check_vma=False,
    )
```

```python
import functools

import jax
import jax.numpy as jnp
from jax import lax
from jax.experimental import pallas as pl
from jax.experimental.pallas import tpu as pltpu
from jax.sharding import PartitionSpec as P

decay_rate = 0.5
eps_one = 1e-30
eps_two = 0.001
learn_rate = 0.01
clip_level = 1.0

MESH = pl.DeviceIdType.MESH
f32 = jnp.float32
PA, PB, PC, PD, PX, PE = range(6)
PIECES = (2, 1, 2, 2, 4, 2)


def exchange_kernel(sizes, grad_hbm, weight_hbm, rowm_hbm, colm_hbm,
                    full, held, col_all, row_new, row_scale, col_scale, scal,
                    own, s_opp, s_right, s_left, r_opp, r_left, r_right, lanes,
                    rowm, colm, col_old, col_parts, sums_yx, sums_zr,
                    load_sem, send_sem, recv_sem, xs_sem, xr_sem, ready):
    rows_all, cols_all = sizes
    rows, width = own.shape[1], own.shape[2]
    half = rows // 2
    entries = float(rows_all) * float(cols_all)
    y, r, c = lax.axis_index("dp"), lax.axis_index("row"), lax.axis_index("col")
    x, z = c // 4, lax.rem(c, 4)
    right, opp, left = lax.rem(y + 1, 4), lax.rem(y + 2, 4), lax.rem(y + 3, 4)

    loads = {}
    def first_rows(i):
        step = half // PIECES[PA]
        return pl.ds((i % 2) * half + (0 if i < 2 else step), step if i < 2 else half - step)

    cols = pl.ds(pl.multiple_of(opp * width, 128), width)
    firsts = [pltpu.make_async_copy(
        grad_hbm.at[0, first_rows(i), cols], own.at[2, first_rows(i)], load_sem.at[(2, 10, 11, 12)[i]]) for i in range(4)]
    for slot, q in ((1, right), (3, left), (0, y)):
        loads[slot] = pltpu.make_async_copy(
            grad_hbm.at[0, :, pl.ds(pl.multiple_of(q * width, 128), width)], own.at[slot], load_sem.at[slot])
    for q in range(4):
        loads[4 + q] = pltpu.make_async_copy(
            weight_hbm.at[:, pl.ds(q * width, width)], held.at[q], load_sem.at[4 + q])
    loads[8] = pltpu.make_async_copy(rowm_hbm, rowm, load_sem.at[8])
    loads[9] = pltpu.make_async_copy(colm_hbm, colm, load_sem.at[9])

    barrier = pltpu.get_barrier_semaphore()
    place = z * 4 + r

    def greet(sem, later):
        sign = 1 if later else -1
        for d in range(1, 4):
            for which, at in (("x", x), ("z", z), ("r", r)):
                to = at + sign * d

                @pl.when((to < 4) if later else (to >= 0))
                def _():
                    for i in range(4 if which == "z" else 1):
                        if which == "x":
                            dev = {"col": to * 4 + z}
                        elif which == "z":
                            dev = {"col": x * 4 + to, "row": i}
                        else:
                            dev = {"row": to}
                        pl.semaphore_signal(sem, inc=1, device_id=dev, device_id_type=MESH)

    for copy in firsts:
        copy.start()
    for q in (right, left, opp):
        pl.semaphore_signal(barrier, inc=1, device_id={"dp": q}, device_id_type=MESH)
    greet(barrier, True)

    def at(phase, h, k):
        step = half // PIECES[phase]
        return pl.ds(h * half + k * step, step)

    def bulk(phase, d, k=0):
        if phase == PA:
            src, dst = s_opp.at[at(phase, d, k)], r_opp.at[at(phase, d, k)]
        elif phase in (PB, PC):
            h = d if phase == PC else 1 - d
            src, dst = ((s_right, r_left), (s_left, r_right))[d]
            src, dst = src.at[at(phase, h, k)], dst.at[at(phase, h, k)]
        else:
            h = 1 - d if phase == PX else d
            q = y if phase != PE else (left, right)[d]
            src = dst = full.at[q, at(phase, h, k)]
        return pltpu.make_async_remote_copy(
            src_ref=src, dst_ref=dst, send_sem=send_sem.at[phase, d, k], recv_sem=recv_sem.at[phase, d, k],
            device_id={"dp": (right, left)[d]}, device_id_type=MESH)

    def arrive(phase, d, k=0):
        if phase < PD:
            bulk(phase, d, k).wait_recv()
            return
        h = 1 - d if phase == PX else d
        q = (left, right)[d] if phase != PE else opp
        ref = full.at[q, at(phase, h, k)]
        pltpu.make_async_remote_copy(
            src_ref=ref, dst_ref=ref, send_sem=send_sem.at[phase, d, k], recv_sem=recv_sem.at[phase, d, k],
            device_id={"dp": (right, left)[d]}, device_id_type=MESH).wait_recv()

    def sent(phase):
        for k in range(PIECES[phase]):
            for d in range(2):
                bulk(phase, d, k).wait_send()

    for k in range(PIECES[PA]):
        for copy in (firsts[:2], firsts[2:], (), ())[k]:
            copy.wait()
        for d in range(2):
            span = at(PA, d, k)
            s_opp[span] = own[2, span].astype(f32)
        if k == 0:
            pl.semaphore_wait(barrier, 3 + x + place)
        for d in range(2):
            bulk(PA, d, k).start()
    for i in (1, 3, 0, 4, 5, 6, 7, 8, 9):
        loads[i].start()
    loads[1].wait()
    loads[3].wait()
    for d, (dst, slot) in enumerate(((s_right, 1), (s_left, 3))):
        span = at(PB, 1 - d, 0)
        dst[span] = own[slot, span].astype(f32)
        bulk(PB, d).start()
    greet(ready, False)
    for i in (0, 4, 5, 6, 7, 8, 9):
        loads[i].wait()

    def weight_step(i, acc):
        w = held[y, pl.ds(pl.multiple_of(i * 8, 8), 8)]
        sq = w * w
        for j in range(width // 128):
            acc = acc + sq[:, j * 128:(j + 1) * 128]
        return acc

    w_lanes = lax.fori_loop(0, rows // 8, weight_step, jnp.zeros((8, 128), f32), unroll=2)
    weight_sums = jnp.sum(w_lanes, axis=0, keepdims=True)
    col_old[...] = colm[...].reshape(col_old.shape)
    mine = pl.ds(pl.multiple_of(y * width, 128), width)
    row_old = rowm[...].reshape(1, rows)
    for k in range(PIECES[PC]):
        for d, (dst, slot) in enumerate(((s_right, 1), (s_left, 3))):
            span = at(PC, d, k)
            arrive(PA, d, k)
            dst[span] = r_opp[span] + own[slot, span].astype(f32)
            bulk(PC, d, k).start()
    sent(PA)
    col_acc = jnp.zeros((8, width), f32)
    arrive(PB, 0)
    arrive(PB, 1)
    for k in range(PIECES[PC]):
        for d in range(2):
            span = at(PC, d, k)
            arrive(PC, d, k)
            g = own[0, span].astype(f32) + r_left[span] + r_right[span]
            full[y, span] = g
            bulk(PD, d, k).start()
            sq = g * g
            for i in range(sq.shape[0] // 8):
                col_acc = col_acc + sq[i * 8:(i + 1) * 8]
            part = sq[:, :128]
            for j in range(1, width // 128):
                part = part + sq[:, j * 128:(j + 1) * 128]
            lanes[span] = part

    def send_small(stage, parts, at, devs):
        ref = parts.at[at]
        for i, dev in devs:
            @pl.when(at != i)
            def _():
                pltpu.make_async_remote_copy(
                    src_ref=ref, dst_ref=ref, send_sem=xs_sem.at[stage], recv_sem=xr_sem.at[stage],
                    device_id=dev, device_id_type=MESH).start()

    def whole(stage, parts, dev):
        rest = parts.at[pl.ds(0, parts.shape[0] - 1)]
        return pltpu.make_async_remote_copy(
            src_ref=rest, dst_ref=rest, send_sem=xs_sem.at[stage], recv_sem=xr_sem.at[stage],
            device_id=dev, device_id_type=MESH)

    def total(parts):
        out = parts[0]
        for i in range(1, parts.shape[0]):
            out = out + parts[i]
        return out

    near = {"row": lax.rem(r + 1, 4)}
    later = 3 - x + 15 - place

    @pl.when(later > 0)
    def _():
        pl.semaphore_wait(ready, later)

    def others(first, last):
        for k in range(first, last):
            for d in range(2):
                bulk(PX, d, k).start()

    col_parts[r] = jnp.sum(col_acc, axis=0, keepdims=True)
    send_small(0, col_parts, r, [(i, {"row": i}) for i in range(4)])
    others(0, 1)
    row_sums = jnp.sum(lanes[...].T, axis=0, keepdims=True)
    old = decay_rate * col_old[:, mine]
    whole(0, col_parts, near).wait_recv()
    col_mine = old + (1.0 - decay_rate) * (total(col_parts) / rows_all + eps_one)
    inverse = 1.0 / col_mine

    def raw_step(k, _):
        span = pl.ds(pl.multiple_of(k * 8, 8), 8)
        g = full[y, span]
        sq = g * g * inverse
        part = sq[:, :128]
        for j in range(1, width // 128):
            part = part + sq[:, j * 128:(j + 1) * 128]
        lanes[span] = part
        return 0

    lax.fori_loop(0, rows // 8, raw_step, 0, unroll=4)
    raw_sums = jnp.sum(lanes[...].T, axis=0, keepdims=True)
    sums_yx[y * 4 + x] = jnp.concatenate([row_sums, raw_sums, weight_sums, jnp.zeros((5, 128), f32)], axis=0)
    send_small(1, sums_yx, y * 4 + x, [(i * 4 + j, {"dp": i, "col": j * 4 + z}) for i in range(4) for j in range(4)])
    others(1, PIECES[PX])
    col_all[:, mine] = col_mine
    for q in (right, left, opp):
        pltpu.make_async_remote_copy(
            src_ref=col_all.at[:, mine], dst_ref=col_all.at[:, mine], send_sem=xs_sem.at[3],
            recv_sem=xr_sem.at[3], device_id={"dp": q}, device_id_type=MESH).start()
    for k in range(PIECES[PE]):
        for d in range(2):
            arrive(PD, d, k)
            bulk(PE, d, k).start()
    whole(1, sums_yx, {"dp": right}).wait_recv()
    sums_zr[place] = jnp.concatenate([total(sums_yx)[0:3], row_old, jnp.zeros((4, 128), f32)], axis=0)
    send_small(2, sums_zr, place, [(i * 4 + j, {"col": x * 4 + i, "row": j}) for i in range(4) for j in range(4)])
    cols_rest = col_all.at[:, pl.ds(0, 3 * width)]
    cols = pltpu.make_async_remote_copy(
        src_ref=cols_rest, dst_ref=cols_rest, send_sem=xs_sem.at[3], recv_sem=xr_sem.at[3],
        device_id={"dp": right}, device_id_type=MESH)
    cols.wait()
    col_scale[...] = lax.rsqrt(col_all[...])
    whole(0, col_parts, near).wait_send()
    whole(1, sums_yx, {"dp": right}).wait_send()
    for phase in (PB, PC, PD, PX):
        sent(phase)
    for k in range(PIECES[PX]):
        for d in range(2):
            arrive(PX, d, k)
    last = PIECES[PE] - 1
    for k in range(last):
        for d in range(2):
            bulk(PE, d, k).wait_send()
            arrive(PE, d, k)
    whole(2, sums_zr, near).wait_recv()

    def moments(group):
        tile = sums_zr[group]
        for i in range(1, 4):
            tile = tile + sums_zr[i * 4 + group]
        return tile, (decay_rate * 0.25) * tile[3:4] + (1.0 - decay_rate) * (tile[0:1] / cols_all + eps_one)

    _, row_mine = moments(r)
    row_new[...] = row_mine
    row_scale[...] = jnp.broadcast_to(lax.rsqrt(row_mine), (128, 128)).T
    sums = [jnp.zeros((1, 128), f32)] * 3
    for group in range(4):
        tile, row_one = moments(group)
        for i, part in enumerate((tile[1:2] / row_one, row_one, tile[2:3])):
            sums[i] = sums[i] + part
    sums = jnp.sum(jnp.concatenate(sums, axis=0), axis=1, keepdims=True)
    row_mean = sums[1:2] / rows_all
    clip = jnp.maximum(1.0, jnp.sqrt(sums[0:1] * row_mean / entries) / clip_level)
    size = learn_rate * jnp.maximum(eps_two, jnp.sqrt(sums[2:3] / entries))
    scal[...] = jnp.concatenate(
        [jnp.broadcast_to(v, (1, 128)) for v in (clip, size, jnp.sqrt(row_mean) / clip, clip)], axis=0)
    for d in range(2):
        bulk(PE, d, last).wait_send()
        arrive(PE, d, last)
    whole(2, sums_zr, near).wait_send()


def update_kernel(full, held, col_all, row_new, row_scale, col_scale, scal,
                  weight_out, update_out, row_out, col_out, clip_out,
                  new_weight, update, row_flat, col_flat, clip_flat, sem, small_sem):
    rows, width = full.shape[1], full.shape[2]
    row_flat[...] = row_new[...].reshape(row_flat.shape)
    col_flat[...] = col_all[...].reshape(col_flat.shape)
    clip_flat[...] = scal[0:1, 0:1]
    size, factor = scal[1:2, :], scal[2:3, :]
    step = 16
    copies = [pltpu.make_async_copy(src, dst, small_sem.at[i]) for i, (src, dst) in enumerate(
        ((row_flat, row_out), (col_flat, col_out), (clip_flat, clip_out)))]
    for copy in copies:
        copy.start()
    for k in range(rows // step):
        for i in range(step // 8):
            at = pl.ds(k * step + i * 8, 8)
            by_row = row_scale[at] * factor
            for q in range(4):
                for j in range(width // 128):
                    col = pl.ds(j * 128, 128)
                    out = pl.ds(q * width + j * 128, 128)
                    u = full[q, at, col] * by_row * col_scale[:, out]
                    update[at, out] = u
                    new_weight[at, out] = held[q, at, col] - size * u
        at = pl.ds(k * step, step)
        for which, (src, dst) in enumerate(((update, update_out), (new_weight, weight_out))):
            copies.append(pltpu.make_async_copy(src.at[at], dst.at[at], sem.at[which, k]))
            copies[-1].start()
    for copy in copies:
        copy.wait()


def solution(mesh):
    assert all(mesh.shape[axis] == size for axis, size in (("dp", 4), ("row", 4), ("col", 16)))

    def body(weight, grad_parts, row_moment, col_moment):
        rows, cols = weight.shape
        width = cols // 4
        vmem = pl.BlockSpec(memory_space=pltpu.VMEM)
        hbm = pl.BlockSpec(memory_space=pltpu.HBM)
        shapes = ((4, rows, width), (4, rows, width), (1, cols), (1, rows), (rows, 128), (1, cols), (4, 128))
        outs = pl.pallas_call(
            functools.partial(exchange_kernel, (rows * 4, cols * 16)),
            out_shape=tuple(pltpu.VMEM(s, f32) for s in shapes),
            in_specs=[hbm] * 4,
            out_specs=(vmem,) * len(shapes),
            scratch_shapes=[
                pltpu.VMEM((4, rows, width), jnp.bfloat16),
                *[pltpu.VMEM((rows, width), f32) for _ in range(6)],
                pltpu.VMEM((rows, 128), f32),
                pltpu.VMEM((rows,), f32),
                pltpu.VMEM((cols,), f32),
                pltpu.VMEM((1, cols), f32),
                pltpu.VMEM((4, 1, width), f32),
                pltpu.VMEM((16, 8, 128), f32),
                pltpu.VMEM((16, 8, 128), f32),
                pltpu.SemaphoreType.DMA((13,)),
                pltpu.SemaphoreType.DMA((6, 2, max(PIECES))),
                pltpu.SemaphoreType.DMA((6, 2, max(PIECES))),
                pltpu.SemaphoreType.DMA((4,)),
                pltpu.SemaphoreType.DMA((4,)),
                pltpu.SemaphoreType.REGULAR,
            ],
            compiler_params=pltpu.CompilerParams(
                collective_id=0, has_side_effects=True, vmem_limit_bytes=24 << 20),
            name="exchange",
        )(*(pltpu.with_memory_space_constraint(a, pltpu.HBM) for a in (grad_parts, weight, row_moment, col_moment)))
        new_weight, update, row_new, col_new, clip = pl.pallas_call(
            update_kernel,
            out_shape=(
                jax.ShapeDtypeStruct((rows, cols), f32),
                jax.ShapeDtypeStruct((rows, cols), f32),
                jax.ShapeDtypeStruct((rows,), f32),
                jax.ShapeDtypeStruct((cols,), f32),
                jax.ShapeDtypeStruct((1, 1), f32),
            ),
            in_specs=[vmem] * len(shapes),
            out_specs=(pl.BlockSpec(memory_space=pl.ANY),) * 5,
            scratch_shapes=[
                pltpu.VMEM((rows, cols), f32),
                pltpu.VMEM((rows, cols), f32),
                pltpu.VMEM((rows,), f32),
                pltpu.VMEM((cols,), f32),
                pltpu.VMEM((1, 1), f32),
                pltpu.SemaphoreType.DMA((2, rows // 16)),
                pltpu.SemaphoreType.DMA((3,)),
            ],
            compiler_params=pltpu.CompilerParams(vmem_limit_bytes=24 << 20),
            name="apply",
        )(*outs)
        return new_weight, update, row_new, col_new, clip.reshape(())

    return jax.shard_map(
        body,
        mesh=mesh,
        in_specs=(P("row", "col"), P("dp", "row", "col"), P("row"), P("col")),
        out_specs=(P("row", "col"), P("row", "col"), P("row"), P("col"), P()),
        check_vma=False,
    )
```

```python
import functools

import jax
import jax.numpy as jnp
from jax import lax
from jax.experimental import pallas as pl
from jax.experimental.pallas import tpu as pltpu
from jax.sharding import PartitionSpec as P

decay_rate = 0.5
eps_one = 1e-30
eps_two = 0.001
learn_rate = 0.01
clip_level = 1.0

MESH = pl.DeviceIdType.MESH
f32 = jnp.float32
PA, PB, PC, PD, PX, PE = range(6)
EARLY = 24
PIECES = (2, 1, 2, 2, 2, 2)


def exchange_kernel(sizes, grad_hbm, weight_hbm, rowm_hbm, colm_hbm,
                    full, held, col_all, row_new, row_scale, col_scale, scal,
                    own, s_opp, s_right, s_left, r_opp, r_left, r_right, lanes,
                    rowm, colm, col_old, col_parts, sums_yx, sums_zr,
                    load_sem, send_sem, recv_sem, xs_sem, xr_sem, ready):
    rows_all, cols_all = sizes
    rows, width = own.shape[1], own.shape[2]
    half = rows // 2
    entries = float(rows_all) * float(cols_all)
    y, r, c = lax.axis_index("dp"), lax.axis_index("row"), lax.axis_index("col")
    x, z = c // 4, lax.rem(c, 4)
    right, opp, left = lax.rem(y + 1, 4), lax.rem(y + 2, 4), lax.rem(y + 3, 4)

    loads = {}
    def first_rows(i):
        step = half // PIECES[PA]
        return pl.ds((i % 2) * half + (0 if i < 2 else step), step if i < 2 else half - step)

    cols = pl.ds(pl.multiple_of(opp * width, 128), width)
    firsts = [pltpu.make_async_copy(
        grad_hbm.at[0, first_rows(i), cols], own.at[2, first_rows(i)], load_sem.at[(2, 10, 11, 12)[i]]) for i in range(4)]
    for slot, q in ((1, right), (3, left), (0, y)):
        loads[slot] = pltpu.make_async_copy(
            grad_hbm.at[0, :, pl.ds(pl.multiple_of(q * width, 128), width)], own.at[slot], load_sem.at[slot])
    for q in range(4):
        loads[4 + q] = pltpu.make_async_copy(
            weight_hbm.at[:, pl.ds(q * width, width)], held.at[q], load_sem.at[4 + q])
    loads[8] = pltpu.make_async_copy(rowm_hbm, rowm, load_sem.at[8])
    loads[9] = pltpu.make_async_copy(colm_hbm, colm, load_sem.at[9])

    barrier = pltpu.get_barrier_semaphore()
    place = z * 4 + r
    hub = 1
    behind = lax.rem(place + 16 - hub, 16)

    def along_x(sem):
        for i in range(1, 4):
            pl.semaphore_signal(sem, inc=1, device_id={"col": i * 4 + z}, device_id_type=MESH)

    def along_z(sem):
        for i in reversed(range(16)):
            if i != hub:
                pl.semaphore_signal(sem, inc=1, device_id={"col": x * 4 + i // 4, "row": i % 4}, device_id_type=MESH)

    def answer():
        @pl.when(x > 0)
        def _():
            pl.semaphore_signal(ready.at[0], inc=1, device_id={"col": z}, device_id_type=MESH)

        @pl.when(behind > 0)
        def _():
            pl.semaphore_signal(
                ready.at[1], inc=1, device_id={"col": x * 4 + hub // 4, "row": hub % 4}, device_id_type=MESH)

    def tell():
        @pl.when(x == 0)
        def _():
            pl.semaphore_wait(ready.at[0], 3)
            along_x(ready.at[0])

        @pl.when(behind == 0)
        def _():
            pl.semaphore_wait(ready.at[1], 15)
            along_z(ready.at[1])

    def told():
        @pl.when(x > 0)
        def _():
            pl.semaphore_wait(ready.at[0], 1)

        @pl.when(behind > 0)
        def _():
            pl.semaphore_wait(ready.at[1], 1)

    for q in (right, left):
        pl.semaphore_signal(barrier, inc=1, device_id={"dp": q}, device_id_type=MESH)
    for copy in firsts[:2]:
        copy.start()
    pl.semaphore_signal(barrier, inc=1, device_id={"dp": opp}, device_id_type=MESH)
    for copy in firsts[2:]:
        copy.start()
    pl.when(x == 0)(lambda: along_x(barrier))
    pl.when(behind == 0)(lambda: along_z(barrier))

    def at(phase, h, k):
        if phase == PX:
            return pl.ds(h * half + (0, EARLY)[k], (EARLY, half - EARLY)[k])
        step = half // PIECES[phase]
        return pl.ds(h * half + k * step, step)

    def bulk(phase, d, k=0):
        if phase == PA:
            src, dst = s_opp.at[at(phase, d, k)], r_opp.at[at(phase, d, k)]
        elif phase in (PB, PC):
            h = d if phase == PC else 1 - d
            src, dst = ((s_right, r_left), (s_left, r_right))[d]
            src, dst = src.at[at(phase, h, k)], dst.at[at(phase, h, k)]
        else:
            h = 1 - d if phase == PX else d
            q = y if phase != PE else (left, right)[d]
            src = dst = full.at[q, at(phase, h, k)]
        return pltpu.make_async_remote_copy(
            src_ref=src, dst_ref=dst, send_sem=send_sem.at[phase, d, k], recv_sem=recv_sem.at[phase, d, k],
            device_id={"dp": (right, left)[d]}, device_id_type=MESH)

    def arrive(phase, d, k=0):
        if phase < PD:
            bulk(phase, d, k).wait_recv()
            return
        h = 1 - d if phase == PX else d
        q = (left, right)[d] if phase != PE else opp
        ref = full.at[q, at(phase, h, k)]
        pltpu.make_async_remote_copy(
            src_ref=ref, dst_ref=ref, send_sem=send_sem.at[phase, d, k], recv_sem=recv_sem.at[phase, d, k],
            device_id={"dp": (right, left)[d]}, device_id_type=MESH).wait_recv()

    def sent(phase):
        for k in range(PIECES[phase]):
            for d in range(2):
                bulk(phase, d, k).wait_send()

    for k in range(PIECES[PA]):
        for copy in (firsts[:2], firsts[2:], (), ())[k]:
            copy.wait()
        for d in range(2):
            span = at(PA, d, k)
            s_opp[span] = own[2, span].astype(f32)
        if k == 0:
            pl.semaphore_wait(barrier, 3 + (x + 3) // 4 + (behind + 15) // 16)
        for d in range(2):
            bulk(PA, d, k).start()
    for i in (1, 3, 0, 4, 5, 6, 7, 8, 9):
        loads[i].start()
    loads[1].wait()
    loads[3].wait()
    for d, (dst, slot) in enumerate(((s_right, 1), (s_left, 3))):
        span = at(PB, 1 - d, 0)
        dst[span] = own[slot, span].astype(f32)
        bulk(PB, d).start()
    answer()
    for i in (0, 4, 5, 6, 7, 8, 9):
        loads[i].wait()

    def weight_step(i, acc):
        w = held[y, pl.ds(pl.multiple_of(i * 8, 8), 8)]
        sq = w * w
        for j in range(width // 128):
            acc = acc + sq[:, j * 128:(j + 1) * 128]
        return acc

    w_lanes = lax.fori_loop(0, rows // 8, weight_step, jnp.zeros((8, 128), f32), unroll=2)
    weight_sums = jnp.sum(w_lanes, axis=0, keepdims=True)
    col_old[...] = colm[...].reshape(col_old.shape)
    mine = pl.ds(pl.multiple_of(y * width, 128), width)
    row_old = rowm[...].reshape(1, rows)
    for k in range(PIECES[PC]):
        for d, (dst, slot) in enumerate(((s_right, 1), (s_left, 3))):
            span = at(PC, d, k)
            arrive(PA, d, k)
            dst[span] = r_opp[span] + own[slot, span].astype(f32)
            bulk(PC, d, k).start()
    sent(PA)
    tell()
    col_acc = jnp.zeros((8, width), f32)
    arrive(PB, 0)
    arrive(PB, 1)
    for k in range(PIECES[PC]):
        for d in range(2):
            span = at(PC, d, k)
            arrive(PC, d, k)
            g = own[0, span].astype(f32) + r_left[span] + r_right[span]
            full[y, span] = g
            bulk(PD, d, k).start()
            sq = g * g
            for i in range(sq.shape[0] // 8):
                col_acc = col_acc + sq[i * 8:(i + 1) * 8]
            part = sq[:, :128]
            for j in range(1, width // 128):
                part = part + sq[:, j * 128:(j + 1) * 128]
            lanes[span] = part

    def send_small(stage, parts, at, devs):
        ref = parts.at[at]
        for i, dev in devs:
            @pl.when(at != i)
            def _():
                pltpu.make_async_remote_copy(
                    src_ref=ref, dst_ref=ref, send_sem=xs_sem.at[stage], recv_sem=xr_sem.at[stage],
                    device_id=dev, device_id_type=MESH).start()

    def whole(stage, parts, dev):
        rest = parts.at[pl.ds(0, parts.shape[0] - 1)]
        return pltpu.make_async_remote_copy(
            src_ref=rest, dst_ref=rest, send_sem=xs_sem.at[stage], recv_sem=xr_sem.at[stage],
            device_id=dev, device_id_type=MESH)

    def total(parts):
        out = parts[0]
        for i in range(1, parts.shape[0]):
            out = out + parts[i]
        return out

    near = {"row": lax.rem(r + 1, 4)}
    told()

    def others(first, last):
        for k in range(first, last):
            for d in range(2):
                bulk(PX, d, k).start()

    col_parts[r] = jnp.sum(col_acc, axis=0, keepdims=True)
    send_small(0, col_parts, r, [(i, {"row": i}) for i in range(4)])
    others(0, 1)
    row_sums = jnp.sum(lanes[...].T, axis=0, keepdims=True)
    old = decay_rate * col_old[:, mine]
    whole(0, col_parts, near).wait_recv()
    col_mine = old + (1.0 - decay_rate) * (total(col_parts) / rows_all + eps_one)
    inverse = 1.0 / col_mine

    def raw_step(k, _):
        span = pl.ds(pl.multiple_of(k * 8, 8), 8)
        g = full[y, span]
        sq = g * g * inverse
        part = sq[:, :128]
        for j in range(1, width // 128):
            part = part + sq[:, j * 128:(j + 1) * 128]
        lanes[span] = part
        return 0

    lax.fori_loop(0, rows // 8, raw_step, 0, unroll=4)
    raw_sums = jnp.sum(lanes[...].T, axis=0, keepdims=True)
    sums_yx[y * 4 + x] = jnp.concatenate([row_sums, raw_sums, weight_sums, jnp.zeros((5, 128), f32)], axis=0)
    send_small(1, sums_yx, y * 4 + x, [(i * 4 + j, {"dp": i, "col": j * 4 + z}) for i in range(4) for j in range(4)])
    others(1, PIECES[PX])
    for k in range(PIECES[PE]):
        for d in range(2):
            arrive(PD, d, k)
            bulk(PE, d, k).start()
    col_all[:, mine] = col_mine
    for q in (right, left, opp):
        pltpu.make_async_remote_copy(
            src_ref=col_all.at[:, mine], dst_ref=col_all.at[:, mine], send_sem=xs_sem.at[3],
            recv_sem=xr_sem.at[3], device_id={"dp": q}, device_id_type=MESH).start()
    whole(1, sums_yx, {"dp": right}).wait_recv()
    sums_zr[place] = jnp.concatenate([total(sums_yx)[0:3], row_old, jnp.zeros((4, 128), f32)], axis=0)
    send_small(2, sums_zr, place, [(i * 4 + j, {"col": x * 4 + i, "row": j}) for i in range(4) for j in range(4)])
    cols_rest = col_all.at[:, pl.ds(0, 3 * width)]
    cols = pltpu.make_async_remote_copy(
        src_ref=cols_rest, dst_ref=cols_rest, send_sem=xs_sem.at[3], recv_sem=xr_sem.at[3],
        device_id={"dp": right}, device_id_type=MESH)
    cols.wait()
    col_scale[...] = lax.rsqrt(col_all[...])
    whole(0, col_parts, near).wait_send()
    whole(1, sums_yx, {"dp": right}).wait_send()
    for phase in (PB, PC, PD, PX):
        sent(phase)
    for k in range(PIECES[PX]):
        for d in range(2):
            arrive(PX, d, k)
    last = PIECES[PE] - 1
    for k in range(last):
        for d in range(2):
            bulk(PE, d, k).wait_send()
            arrive(PE, d, k)
    whole(2, sums_zr, near).wait_recv()

    def moments(group):
        tile = sums_zr[group]
        for i in range(1, 4):
            tile = tile + sums_zr[i * 4 + group]
        return tile, (decay_rate * 0.25) * tile[3:4] + (1.0 - decay_rate) * (tile[0:1] / cols_all + eps_one)

    _, row_mine = moments(r)
    row_new[...] = row_mine
    row_scale[...] = jnp.broadcast_to(lax.rsqrt(row_mine), (128, 128)).T
    sums = [jnp.zeros((1, 128), f32)] * 3
    for group in range(4):
        tile, row_one = moments(group)
        for i, part in enumerate((tile[1:2] / row_one, row_one, tile[2:3])):
            sums[i] = sums[i] + part
    sums = jnp.sum(jnp.concatenate(sums, axis=0), axis=1, keepdims=True)
    row_mean = sums[1:2] / rows_all
    clip = jnp.maximum(1.0, jnp.sqrt(sums[0:1] * row_mean / entries) / clip_level)
    size = learn_rate * jnp.maximum(eps_two, jnp.sqrt(sums[2:3] / entries))
    scal[...] = jnp.concatenate(
        [jnp.broadcast_to(v, (1, 128)) for v in (clip, size, jnp.sqrt(row_mean) / clip, clip)], axis=0)
    for d in range(2):
        bulk(PE, d, last).wait_send()
        arrive(PE, d, last)
    whole(2, sums_zr, near).wait_send()


def update_kernel(full, held, col_all, row_new, row_scale, col_scale, scal,
                  weight_out, update_out, row_out, col_out, clip_out,
                  new_weight, update, row_flat, col_flat, clip_flat, sem, small_sem):
    rows, width = full.shape[1], full.shape[2]
    row_flat[...] = row_new[...].reshape(row_flat.shape)
    col_flat[...] = col_all[...].reshape(col_flat.shape)
    clip_flat[...] = scal[0:1, 0:1]
    size, factor = scal[1:2, :], scal[2:3, :]
    step = 16
    copies = [pltpu.make_async_copy(src, dst, small_sem.at[i]) for i, (src, dst) in enumerate(
        ((row_flat, row_out), (col_flat, col_out), (clip_flat, clip_out)))]
    for copy in copies:
        copy.start()
    for k in range(rows // step):
        for i in range(step // 8):
            at = pl.ds(k * step + i * 8, 8)
            by_row = row_scale[at] * factor
            for q in range(4):
                for j in range(width // 128):
                    col = pl.ds(j * 128, 128)
                    out = pl.ds(q * width + j * 128, 128)
                    u = full[q, at, col] * by_row * col_scale[:, out]
                    update[at, out] = u
                    new_weight[at, out] = held[q, at, col] - size * u
        at = pl.ds(k * step, step)
        for which, (src, dst) in enumerate(((update, update_out), (new_weight, weight_out))):
            copies.append(pltpu.make_async_copy(src.at[at], dst.at[at], sem.at[which, k]))
            copies[-1].start()
    for copy in copies:
        copy.wait()


def solution(mesh):
    assert all(mesh.shape[axis] == size for axis, size in (("dp", 4), ("row", 4), ("col", 16)))

    def body(weight, grad_parts, row_moment, col_moment):
        rows, cols = weight.shape
        width = cols // 4
        vmem = pl.BlockSpec(memory_space=pltpu.VMEM)
        hbm = pl.BlockSpec(memory_space=pltpu.HBM)
        shapes = ((4, rows, width), (4, rows, width), (1, cols), (1, rows), (rows, 128), (1, cols), (4, 128))
        outs = pl.pallas_call(
            functools.partial(exchange_kernel, (rows * 4, cols * 16)),
            out_shape=tuple(pltpu.VMEM(s, f32) for s in shapes),
            in_specs=[hbm] * 4,
            out_specs=(vmem,) * len(shapes),
            scratch_shapes=[
                pltpu.VMEM((4, rows, width), jnp.bfloat16),
                *[pltpu.VMEM((rows, width), f32) for _ in range(6)],
                pltpu.VMEM((rows, 128), f32),
                pltpu.VMEM((rows,), f32),
                pltpu.VMEM((cols,), f32),
                pltpu.VMEM((1, cols), f32),
                pltpu.VMEM((4, 1, width), f32),
                pltpu.VMEM((16, 8, 128), f32),
                pltpu.VMEM((16, 8, 128), f32),
                pltpu.SemaphoreType.DMA((13,)),
                pltpu.SemaphoreType.DMA((6, 2, max(PIECES))),
                pltpu.SemaphoreType.DMA((6, 2, max(PIECES))),
                pltpu.SemaphoreType.DMA((4,)),
                pltpu.SemaphoreType.DMA((4,)),
                pltpu.SemaphoreType.REGULAR((2,)),
            ],
            compiler_params=pltpu.CompilerParams(
                collective_id=0, has_side_effects=True, vmem_limit_bytes=24 << 20),
            name="exchange",
        )(*(pltpu.with_memory_space_constraint(a, pltpu.HBM) for a in (grad_parts, weight, row_moment, col_moment)))
        new_weight, update, row_new, col_new, clip = pl.pallas_call(
            update_kernel,
            out_shape=(
                jax.ShapeDtypeStruct((rows, cols), f32),
                jax.ShapeDtypeStruct((rows, cols), f32),
                jax.ShapeDtypeStruct((rows,), f32),
                jax.ShapeDtypeStruct((cols,), f32),
                jax.ShapeDtypeStruct((1, 1), f32),
            ),
            in_specs=[vmem] * len(shapes),
            out_specs=(pl.BlockSpec(memory_space=pl.ANY),) * 5,
            scratch_shapes=[
                pltpu.VMEM((rows, cols), f32),
                pltpu.VMEM((rows, cols), f32),
                pltpu.VMEM((rows,), f32),
                pltpu.VMEM((cols,), f32),
                pltpu.VMEM((1, 1), f32),
                pltpu.SemaphoreType.DMA((2, rows // 16)),
                pltpu.SemaphoreType.DMA((3,)),
            ],
            compiler_params=pltpu.CompilerParams(vmem_limit_bytes=24 << 20),
            name="apply",
        )(*outs)
        return new_weight, update, row_new, col_new, clip.reshape(())

    return jax.shard_map(
        body,
        mesh=mesh,
        in_specs=(P("row", "col"), P("dp", "row", "col"), P("row"), P("col")),
        out_specs=(P("row", "col"), P("row", "col"), P("row"), P("col"), P()),
        check_vma=False,
    )
```

```python
import functools

import jax
import jax.numpy as jnp
from jax import lax
from jax.experimental import pallas as pl
from jax.experimental.pallas import tpu as pltpu
from jax.sharding import PartitionSpec as P

decay_rate = 0.5
eps_one = 1e-30
eps_two = 0.001
learn_rate = 0.01
clip_level = 1.0

MESH = pl.DeviceIdType.MESH
f32 = jnp.float32
PA, PB, PC, PD, PX, PE = range(6)
EARLY = 24
PIECES = (2, 1, 2, 2, 2, 2)


def exchange_kernel(sizes, grad_hbm, weight_hbm, rowm_hbm, colm_hbm,
                    full, held, col_all, row_new, row_scale, col_scale, scal,
                    own, s_opp, s_right, s_left, r_opp, r_left, r_right, lanes,
                    rowm, colm, col_old, col_parts, sums_yx, sums_zr,
                    load_sem, send_sem, recv_sem, xs_sem, xr_sem, ready):
    rows_all, cols_all = sizes
    rows, width = own.shape[1], own.shape[2]
    half = rows // 2
    entries = float(rows_all) * float(cols_all)
    y, r, c = lax.axis_index("dp"), lax.axis_index("row"), lax.axis_index("col")
    x, z = c // 4, lax.rem(c, 4)
    right, opp, left = lax.rem(y + 1, 4), lax.rem(y + 2, 4), lax.rem(y + 3, 4)

    loads = {}
    def first_rows(i):
        step = half // PIECES[PA]
        return pl.ds((i % 2) * half + (0 if i < 2 else step), step if i < 2 else half - step)

    cols = pl.ds(pl.multiple_of(opp * width, 128), width)
    firsts = [pltpu.make_async_copy(
        grad_hbm.at[0, first_rows(i), cols], own.at[2, first_rows(i)], load_sem.at[(2, 10, 11, 12)[i]]) for i in range(4)]
    for slot, q in ((1, right), (3, left), (0, y)):
        loads[slot] = pltpu.make_async_copy(
            grad_hbm.at[0, :, pl.ds(pl.multiple_of(q * width, 128), width)], own.at[slot], load_sem.at[slot])
    for q in range(4):
        loads[4 + q] = pltpu.make_async_copy(
            weight_hbm.at[:, pl.ds(q * width, width)], held.at[q], load_sem.at[4 + q])
    loads[8] = pltpu.make_async_copy(rowm_hbm, rowm, load_sem.at[8])
    loads[9] = pltpu.make_async_copy(colm_hbm, colm, load_sem.at[9])

    barrier = pltpu.get_barrier_semaphore()
    place = z * 4 + r
    hub = 1
    behind = lax.rem(place + 16 - hub, 16)

    def along_x(sem):
        for i in range(1, 4):
            pl.semaphore_signal(sem, inc=1, device_id={"col": i * 4 + z}, device_id_type=MESH)

    def along_z(sem):
        for i in reversed(range(16)):
            if i != hub:
                pl.semaphore_signal(sem, inc=1, device_id={"col": x * 4 + i // 4, "row": i % 4}, device_id_type=MESH)

    def answer():
        @pl.when(x > 0)
        def _():
            pl.semaphore_signal(ready.at[0], inc=1, device_id={"col": z}, device_id_type=MESH)

        @pl.when(behind > 0)
        def _():
            pl.semaphore_signal(
                ready.at[1], inc=1, device_id={"col": x * 4 + hub // 4, "row": hub % 4}, device_id_type=MESH)

    def tell():
        @pl.when(x == 0)
        def _():
            pl.semaphore_wait(ready.at[0], 3)
            along_x(ready.at[0])

        @pl.when(behind == 0)
        def _():
            pl.semaphore_wait(ready.at[1], 15)
            along_z(ready.at[1])

    def told():
        @pl.when(x > 0)
        def _():
            pl.semaphore_wait(ready.at[0], 1)

        @pl.when(behind > 0)
        def _():
            pl.semaphore_wait(ready.at[1], 1)

    for q in (right, left):
        pl.semaphore_signal(barrier, inc=1, device_id={"dp": q}, device_id_type=MESH)
    for copy in firsts[:2]:
        copy.start()
    pl.semaphore_signal(barrier, inc=1, device_id={"dp": opp}, device_id_type=MESH)
    for copy in firsts[2:]:
        copy.start()
    pl.when(x == 0)(lambda: along_x(barrier))
    pl.when(behind == 0)(lambda: along_z(barrier))

    def at(phase, h, k):
        if phase == PX:
            return pl.ds(h * half + (0, EARLY)[k], (EARLY, half - EARLY)[k])
        step = half // PIECES[phase]
        return pl.ds(h * half + k * step, step)

    def bulk(phase, d, k=0):
        if phase == PA:
            src, dst = s_opp.at[at(phase, d, k)], r_opp.at[at(phase, d, k)]
        elif phase in (PB, PC):
            h = d if phase == PC else 1 - d
            src, dst = ((s_right, r_left), (s_left, r_right))[d]
            src, dst = src.at[at(phase, h, k)], dst.at[at(phase, h, k)]
        else:
            h = 1 - d if phase == PX else d
            q = y if phase != PE else (left, right)[d]
            src = dst = full.at[q, at(phase, h, k)]
        return pltpu.make_async_remote_copy(
            src_ref=src, dst_ref=dst, send_sem=send_sem.at[phase, d, k], recv_sem=recv_sem.at[phase, d, k],
            device_id={"dp": (right, left)[d]}, device_id_type=MESH)

    def arrive(phase, d, k=0):
        if phase < PD:
            bulk(phase, d, k).wait_recv()
            return
        h = 1 - d if phase == PX else d
        q = (left, right)[d] if phase != PE else opp
        ref = full.at[q, at(phase, h, k)]
        pltpu.make_async_remote_copy(
            src_ref=ref, dst_ref=ref, send_sem=send_sem.at[phase, d, k], recv_sem=recv_sem.at[phase, d, k],
            device_id={"dp": (right, left)[d]}, device_id_type=MESH).wait_recv()

    def sent(phase):
        for k in range(PIECES[phase]):
            for d in range(2):
                bulk(phase, d, k).wait_send()

    for k in range(PIECES[PA]):
        for copy in (firsts[:2], firsts[2:], (), ())[k]:
            copy.wait()
        for d in range(2):
            span = at(PA, d, k)
            s_opp[span] = own[2, span].astype(f32)
        if k == 0:
            pl.semaphore_wait(barrier, 3 + (x + 3) // 4 + (behind + 15) // 16)
        for d in range(2):
            bulk(PA, d, k).start()
    for i in (1, 3, 0, 4, 5, 6, 7, 8, 9):
        loads[i].start()
    loads[1].wait()
    loads[3].wait()
    for d, (dst, slot) in enumerate(((s_right, 1), (s_left, 3))):
        span = at(PB, 1 - d, 0)
        dst[span] = own[slot, span].astype(f32)
        bulk(PB, d).start()
    answer()
    for i in (0, 4, 5, 6, 7, 8, 9):
        loads[i].wait()

    def weight_step(i, acc):
        w = held[y, pl.ds(pl.multiple_of(i * 8, 8), 8)]
        sq = w * w
        for j in range(width // 128):
            acc = acc + sq[:, j * 128:(j + 1) * 128]
        return acc

    w_lanes = lax.fori_loop(0, rows // 8, weight_step, jnp.zeros((8, 128), f32), unroll=2)
    weight_sums = jnp.sum(w_lanes, axis=0, keepdims=True)
    col_old[...] = colm[...].reshape(col_old.shape)
    mine = pl.ds(pl.multiple_of(y * width, 128), width)
    row_old = rowm[...].reshape(1, rows)
    for k in range(PIECES[PC]):
        for d, (dst, slot) in enumerate(((s_right, 1), (s_left, 3))):
            span = at(PC, d, k)
            arrive(PA, d, k)
            dst[span] = r_opp[span] + own[slot, span].astype(f32)
            bulk(PC, d, k).start()
    sent(PA)
    tell()
    col_acc = jnp.zeros((8, width), f32)
    arrive(PB, 0)
    arrive(PB, 1)
    for k in range(PIECES[PC]):
        for d in range(2):
            span = at(PC, d, k)
            arrive(PC, d, k)
            g = own[0, span].astype(f32) + r_left[span] + r_right[span]
            full[y, span] = g
            bulk(PD, d, k).start()
            sq = g * g
            for i in range(sq.shape[0] // 8):
                col_acc = col_acc + sq[i * 8:(i + 1) * 8]
            part = sq[:, :128]
            for j in range(1, width // 128):
                part = part + sq[:, j * 128:(j + 1) * 128]
            lanes[span] = part

    def send_small(stage, parts, at, devs):
        ref = parts.at[at]
        for i, dev in devs:
            @pl.when(at != i)
            def _():
                pltpu.make_async_remote_copy(
                    src_ref=ref, dst_ref=ref, send_sem=xs_sem.at[stage], recv_sem=xr_sem.at[stage],
                    device_id=dev, device_id_type=MESH).start()

    def whole(stage, parts, dev):
        rest = parts.at[pl.ds(0, parts.shape[0] - 1)]
        return pltpu.make_async_remote_copy(
            src_ref=rest, dst_ref=rest, send_sem=xs_sem.at[stage], recv_sem=xr_sem.at[stage],
            device_id=dev, device_id_type=MESH)

    def total(parts):
        out = parts[0]
        for i in range(1, parts.shape[0]):
            out = out + parts[i]
        return out

    near = {"row": lax.rem(r + 1, 4)}
    told()

    def others(first, last):
        for k in range(first, last):
            for d in range(2):
                bulk(PX, d, k).start()

    col_parts[r] = jnp.sum(col_acc, axis=0, keepdims=True)
    send_small(0, col_parts, r, [(i, {"row": i}) for i in range(4)])
    others(0, 1)
    row_sums = jnp.sum(lanes[...].T, axis=0, keepdims=True)
    old = decay_rate * col_old[:, mine]
    whole(0, col_parts, near).wait_recv()
    col_mine = old + (1.0 - decay_rate) * (total(col_parts) / rows_all + eps_one)
    inverse = 1.0 / col_mine

    def raw_step(k, _):
        span = pl.ds(pl.multiple_of(k * 8, 8), 8)
        g = full[y, span]
        sq = g * g * inverse
        part = sq[:, :128]
        for j in range(1, width // 128):
            part = part + sq[:, j * 128:(j + 1) * 128]
        lanes[span] = part
        return 0

    lax.fori_loop(0, rows // 8, raw_step, 0, unroll=4)
    raw_sums = jnp.sum(lanes[...].T, axis=0, keepdims=True)
    sums_yx[y * 4 + x] = jnp.concatenate([row_sums, raw_sums, weight_sums, jnp.zeros((1, 128), f32)], axis=0)
    send_small(1, sums_yx, y * 4 + x, [(i * 4 + j, {"dp": i, "col": j * 4 + z}) for i in range(4) for j in range(4)])
    others(1, PIECES[PX])
    for k in range(PIECES[PE]):
        for d in range(2):
            arrive(PD, d, k)
            bulk(PE, d, k).start()
    col_all[:, mine] = col_mine
    for q in (right, left, opp):
        pltpu.make_async_remote_copy(
            src_ref=col_all.at[:, mine], dst_ref=col_all.at[:, mine], send_sem=xs_sem.at[3],
            recv_sem=xr_sem.at[3], device_id={"dp": q}, device_id_type=MESH).start()
    whole(1, sums_yx, {"dp": right}).wait_recv()
    sums_zr[place] = jnp.concatenate([total(sums_yx)[0:3], row_old], axis=0)
    send_small(2, sums_zr, place, [(i * 4 + j, {"col": x * 4 + i, "row": j}) for i in range(4) for j in range(4)])
    cols_rest = col_all.at[:, pl.ds(0, 3 * width)]
    cols = pltpu.make_async_remote_copy(
        src_ref=cols_rest, dst_ref=cols_rest, send_sem=xs_sem.at[3], recv_sem=xr_sem.at[3],
        device_id={"dp": right}, device_id_type=MESH)
    cols.wait()
    col_scale[...] = lax.rsqrt(col_all[...])
    whole(0, col_parts, near).wait_send()
    whole(1, sums_yx, {"dp": right}).wait_send()
    for phase in (PB, PC, PD, PX):
        sent(phase)
    for k in range(PIECES[PX]):
        for d in range(2):
            arrive(PX, d, k)
    last = PIECES[PE] - 1
    for k in range(last):
        for d in range(2):
            bulk(PE, d, k).wait_send()
            arrive(PE, d, k)
    whole(2, sums_zr, near).wait_recv()

    def moments(group):
        tile = sums_zr[group]
        for i in range(1, 4):
            tile = tile + sums_zr[i * 4 + group]
        return tile, (decay_rate * 0.25) * tile[3:4] + (1.0 - decay_rate) * (tile[0:1] / cols_all + eps_one)

    _, row_mine = moments(r)
    row_new[...] = row_mine
    row_scale[...] = jnp.broadcast_to(lax.rsqrt(row_mine), (128, 128)).T
    sums = [jnp.zeros((1, 128), f32)] * 3
    for group in range(4):
        tile, row_one = moments(group)
        for i, part in enumerate((tile[1:2] / row_one, row_one, tile[2:3])):
            sums[i] = sums[i] + part
    sums = jnp.sum(jnp.concatenate(sums, axis=0), axis=1, keepdims=True)
    row_mean = sums[1:2] / rows_all
    clip = jnp.maximum(1.0, jnp.sqrt(sums[0:1] * row_mean / entries) / clip_level)
    size = learn_rate * jnp.maximum(eps_two, jnp.sqrt(sums[2:3] / entries))
    scal[...] = jnp.concatenate(
        [jnp.broadcast_to(v, (1, 128)) for v in (clip, size, jnp.sqrt(row_mean) / clip, clip)], axis=0)
    for d in range(2):
        bulk(PE, d, last).wait_send()
        arrive(PE, d, last)
    whole(2, sums_zr, near).wait_send()


def update_kernel(full, held, col_all, row_new, row_scale, col_scale, scal,
                  weight_out, update_out, row_out, col_out, clip_out,
                  new_weight, update, row_flat, col_flat, clip_flat, sem, small_sem):
    rows, width = full.shape[1], full.shape[2]
    row_flat[...] = row_new[...].reshape(row_flat.shape)
    col_flat[...] = col_all[...].reshape(col_flat.shape)
    clip_flat[...] = scal[0:1, 0:1]
    size, factor = scal[1:2, :], scal[2:3, :]
    step = 16
    copies = [pltpu.make_async_copy(src, dst, small_sem.at[i]) for i, (src, dst) in enumerate(
        ((row_flat, row_out), (col_flat, col_out), (clip_flat, clip_out)))]
    for copy in copies:
        copy.start()
    for k in range(rows // step):
        for i in range(step // 8):
            at = pl.ds(k * step + i * 8, 8)
            by_row = row_scale[at] * factor
            for q in range(4):
                for j in range(width // 128):
                    col = pl.ds(j * 128, 128)
                    out = pl.ds(q * width + j * 128, 128)
                    u = full[q, at, col] * by_row * col_scale[:, out]
                    update[at, out] = u
                    new_weight[at, out] = held[q, at, col] - size * u
        at = pl.ds(k * step, step)
        for which, (src, dst) in enumerate(((update, update_out), (new_weight, weight_out))):
            copies.append(pltpu.make_async_copy(src.at[at], dst.at[at], sem.at[which, k]))
            copies[-1].start()
    for copy in copies:
        copy.wait()


def solution(mesh):
    assert all(mesh.shape[axis] == size for axis, size in (("dp", 4), ("row", 4), ("col", 16)))

    def body(weight, grad_parts, row_moment, col_moment):
        rows, cols = weight.shape
        width = cols // 4
        vmem = pl.BlockSpec(memory_space=pltpu.VMEM)
        hbm = pl.BlockSpec(memory_space=pltpu.HBM)
        shapes = ((4, rows, width), (4, rows, width), (1, cols), (1, rows), (rows, 128), (1, cols), (4, 128))
        outs = pl.pallas_call(
            functools.partial(exchange_kernel, (rows * 4, cols * 16)),
            out_shape=tuple(pltpu.VMEM(s, f32) for s in shapes),
            in_specs=[hbm] * 4,
            out_specs=(vmem,) * len(shapes),
            scratch_shapes=[
                pltpu.VMEM((4, rows, width), jnp.bfloat16),
                *[pltpu.VMEM((rows, width), f32) for _ in range(6)],
                pltpu.VMEM((rows, 128), f32),
                pltpu.VMEM((rows,), f32),
                pltpu.VMEM((cols,), f32),
                pltpu.VMEM((1, cols), f32),
                pltpu.VMEM((4, 1, width), f32),
                pltpu.VMEM((16, 4, 128), f32),
                pltpu.VMEM((16, 4, 128), f32),
                pltpu.SemaphoreType.DMA((13,)),
                pltpu.SemaphoreType.DMA((6, 2, max(PIECES))),
                pltpu.SemaphoreType.DMA((6, 2, max(PIECES))),
                pltpu.SemaphoreType.DMA((4,)),
                pltpu.SemaphoreType.DMA((4,)),
                pltpu.SemaphoreType.REGULAR((2,)),
            ],
            compiler_params=pltpu.CompilerParams(
                collective_id=0, has_side_effects=True, vmem_limit_bytes=24 << 20),
            name="exchange",
        )(*(pltpu.with_memory_space_constraint(a, pltpu.HBM) for a in (grad_parts, weight, row_moment, col_moment)))
        new_weight, update, row_new, col_new, clip = pl.pallas_call(
            update_kernel,
            out_shape=(
                jax.ShapeDtypeStruct((rows, cols), f32),
                jax.ShapeDtypeStruct((rows, cols), f32),
                jax.ShapeDtypeStruct((rows,), f32),
                jax.ShapeDtypeStruct((cols,), f32),
                jax.ShapeDtypeStruct((1, 1), f32),
            ),
            in_specs=[vmem] * len(shapes),
            out_specs=(pl.BlockSpec(memory_space=pl.ANY),) * 5,
            scratch_shapes=[
                pltpu.VMEM((rows, cols), f32),
                pltpu.VMEM((rows, cols), f32),
                pltpu.VMEM((rows,), f32),
                pltpu.VMEM((cols,), f32),
                pltpu.VMEM((1, 1), f32),
                pltpu.SemaphoreType.DMA((2, rows // 16)),
                pltpu.SemaphoreType.DMA((3,)),
            ],
            compiler_params=pltpu.CompilerParams(vmem_limit_bytes=24 << 20),
            name="apply",
        )(*outs)
        return new_weight, update, row_new, col_new, clip.reshape(())

    return jax.shard_map(
        body,
        mesh=mesh,
        in_specs=(P("row", "col"), P("dp", "row", "col"), P("row"), P("col")),
        out_specs=(P("row", "col"), P("row", "col"), P("row"), P("col"), P()),
        check_vma=False,
    )
```

```python
import functools

import jax
import jax.numpy as jnp
from jax import lax
from jax.experimental import pallas as pl
from jax.experimental.pallas import tpu as pltpu
from jax.sharding import PartitionSpec as P

decay_rate = 0.5
eps_one = 1e-30
eps_two = 0.001
learn_rate = 0.01
clip_level = 1.0

MESH = pl.DeviceIdType.MESH
f32 = jnp.float32
PA, PB, PC, PD, PX, PE = range(6)
EARLY = 24
PIECES = (2, 1, 2, 2, 2, 2)


def exchange_kernel(sizes, grad_hbm, weight_hbm, rowm_hbm, colm_hbm,
                    full, held, col_all, row_new, row_scale, col_scale, scal,
                    own, s_opp, s_right, s_left, r_opp, r_left, r_right, lanes,
                    rowm, colm, col_old, col_parts, sums_yx, sums_zr,
                    load_sem, send_sem, recv_sem, xs_sem, xr_sem, ready):
    rows_all, cols_all = sizes
    rows, width = own.shape[1], own.shape[2]
    half = rows // 2
    entries = float(rows_all) * float(cols_all)
    y, r, c = lax.axis_index("dp"), lax.axis_index("row"), lax.axis_index("col")
    x, z = c // 4, lax.rem(c, 4)
    right, opp, left = lax.rem(y + 1, 4), lax.rem(y + 2, 4), lax.rem(y + 3, 4)

    loads = {}
    def first_rows(i):
        step = half // PIECES[PA]
        return pl.ds((i % 2) * half + (0 if i < 2 else step), step if i < 2 else half - step)

    cols = pl.ds(pl.multiple_of(opp * width, 128), width)
    firsts = [pltpu.make_async_copy(
        grad_hbm.at[0, first_rows(i), cols], own.at[2, first_rows(i)], load_sem.at[(2, 10, 11, 12)[i]]) for i in range(4)]
    for slot, q in ((1, right), (3, left), (0, y)):
        loads[slot] = pltpu.make_async_copy(
            grad_hbm.at[0, :, pl.ds(pl.multiple_of(q * width, 128), width)], own.at[slot], load_sem.at[slot])
    for q in range(4):
        loads[4 + q] = pltpu.make_async_copy(
            weight_hbm.at[:, pl.ds(q * width, width)], held.at[q], load_sem.at[4 + q])
    loads[8] = pltpu.make_async_copy(rowm_hbm, rowm, load_sem.at[8])
    loads[9] = pltpu.make_async_copy(colm_hbm, colm, load_sem.at[9])

    barrier = pltpu.get_barrier_semaphore()
    place = z * 4 + r
    hub = 1
    behind = lax.rem(place + 16 - hub, 16)

    def along_x(sem):
        for i in range(1, 4):
            pl.semaphore_signal(sem, inc=1, device_id={"col": i * 4 + z}, device_id_type=MESH)

    def along_z(sem):
        for i in reversed(range(16)):
            if i != hub:
                pl.semaphore_signal(sem, inc=1, device_id={"col": x * 4 + i // 4, "row": i % 4}, device_id_type=MESH)

    def answer():
        @pl.when(x > 0)
        def _():
            pl.semaphore_signal(ready.at[0], inc=1, device_id={"col": z}, device_id_type=MESH)

        @pl.when(behind > 0)
        def _():
            pl.semaphore_signal(
                ready.at[1], inc=1, device_id={"col": x * 4 + hub // 4, "row": hub % 4}, device_id_type=MESH)

    def tell():
        @pl.when(x == 0)
        def _():
            pl.semaphore_wait(ready.at[0], 3)
            along_x(ready.at[0])

        @pl.when(behind == 0)
        def _():
            pl.semaphore_wait(ready.at[1], 15)
            along_z(ready.at[1])

    def told():
        @pl.when(x > 0)
        def _():
            pl.semaphore_wait(ready.at[0], 1)

        @pl.when(behind > 0)
        def _():
            pl.semaphore_wait(ready.at[1], 1)

    for q in (right, left):
        pl.semaphore_signal(barrier, inc=1, device_id={"dp": q}, device_id_type=MESH)
    for copy in firsts[:2]:
        copy.start()
    for copy in firsts[2:]:
        copy.start()
    pl.when(x == 0)(lambda: along_x(barrier))
    pl.when(behind == 0)(lambda: along_z(barrier))

    def at(phase, h, k):
        if phase == PX:
            return pl.ds(h * half + (0, EARLY)[k], (EARLY, half - EARLY)[k])
        step = half // PIECES[phase]
        return pl.ds(h * half + k * step, step)

    def bulk(phase, d, k=0):
        if phase == PA:
            src, dst = s_opp.at[at(phase, d, k)], r_opp.at[at(phase, d, k)]
        elif phase in (PB, PC):
            h = d if phase == PC else 1 - d
            src, dst = ((s_right, r_left), (s_left, r_right))[d]
            src, dst = src.at[at(phase, h, k)], dst.at[at(phase, h, k)]
        else:
            h = 1 - d if phase == PX else d
            q = y if phase != PE else (left, right)[d]
            src = dst = full.at[q, at(phase, h, k)]
        return pltpu.make_async_remote_copy(
            src_ref=src, dst_ref=dst, send_sem=send_sem.at[phase, d, k], recv_sem=recv_sem.at[phase, d, k],
            device_id={"dp": (right, left)[d]}, device_id_type=MESH)

    def arrive(phase, d, k=0):
        if phase < PD:
            bulk(phase, d, k).wait_recv()
            return
        h = 1 - d if phase == PX else d
        q = (left, right)[d] if phase != PE else opp
        ref = full.at[q, at(phase, h, k)]
        pltpu.make_async_remote_copy(
            src_ref=ref, dst_ref=ref, send_sem=send_sem.at[phase, d, k], recv_sem=recv_sem.at[phase, d, k],
            device_id={"dp": (right, left)[d]}, device_id_type=MESH).wait_recv()

    def sent(phase):
        for k in range(PIECES[phase]):
            for d in range(2):
                bulk(phase, d, k).wait_send()

    for k in range(PIECES[PA]):
        for copy in (firsts[:2], firsts[2:], (), ())[k]:
            copy.wait()
        for d in range(2):
            span = at(PA, d, k)
            s_opp[span] = own[2, span].astype(f32)
        if k == 0:
            pl.semaphore_wait(barrier, 2 + (x + 3) // 4 + (behind + 15) // 16)
        for d in range(2):
            bulk(PA, d, k).start()
    for i in (1, 3, 0, 4, 5, 6, 7, 8, 9):
        loads[i].start()
    loads[1].wait()
    loads[3].wait()
    for d, (dst, slot) in enumerate(((s_right, 1), (s_left, 3))):
        span = at(PB, 1 - d, 0)
        dst[span] = own[slot, span].astype(f32)
        bulk(PB, d).start()
    for i in (0, 4, 5, 6, 7, 8, 9):
        loads[i].wait()

    def weight_step(i, acc):
        w = held[y, pl.ds(pl.multiple_of(i * 8, 8), 8)]
        sq = w * w
        for j in range(width // 128):
            acc = acc + sq[:, j * 128:(j + 1) * 128]
        return acc

    w_lanes = lax.fori_loop(0, rows // 8, weight_step, jnp.zeros((8, 128), f32), unroll=2)
    weight_sums = jnp.sum(w_lanes, axis=0, keepdims=True)
    col_old[...] = colm[...].reshape(col_old.shape)
    mine = pl.ds(pl.multiple_of(y * width, 128), width)
    row_old = rowm[...].reshape(1, rows)
    for k in range(PIECES[PC]):
        for d, (dst, slot) in enumerate(((s_right, 1), (s_left, 3))):
            span = at(PC, d, k)
            arrive(PA, d, k)
            dst[span] = r_opp[span] + own[slot, span].astype(f32)
            bulk(PC, d, k).start()
    answer()
    sent(PA)
    tell()
    col_acc = jnp.zeros((8, width), f32)
    arrive(PB, 0)
    arrive(PB, 1)
    for k in range(PIECES[PC]):
        for d in range(2):
            span = at(PC, d, k)
            arrive(PC, d, k)
            g = own[0, span].astype(f32) + r_left[span] + r_right[span]
            full[y, span] = g
            bulk(PD, d, k).start()
            sq = g * g
            for i in range(sq.shape[0] // 8):
                col_acc = col_acc + sq[i * 8:(i + 1) * 8]
            part = sq[:, :128]
            for j in range(1, width // 128):
                part = part + sq[:, j * 128:(j + 1) * 128]
            lanes[span] = part

    def send_small(stage, parts, at, devs):
        ref = parts.at[at]
        for i, dev in devs:
            @pl.when(at != i)
            def _():
                pltpu.make_async_remote_copy(
                    src_ref=ref, dst_ref=ref, send_sem=xs_sem.at[stage], recv_sem=xr_sem.at[stage],
                    device_id=dev, device_id_type=MESH).start()

    def whole(stage, parts, dev):
        rest = parts.at[pl.ds(0, parts.shape[0] - 1)]
        return pltpu.make_async_remote_copy(
            src_ref=rest, dst_ref=rest, send_sem=xs_sem.at[stage], recv_sem=xr_sem.at[stage],
            device_id=dev, device_id_type=MESH)

    def total(parts):
        out = parts[0]
        for i in range(1, parts.shape[0]):
            out = out + parts[i]
        return out

    near = {"row": lax.rem(r + 1, 4)}
    told()

    def others(first, last):
        for k in range(first, last):
            for d in range(2):
                bulk(PX, d, k).start()

    col_parts[r] = jnp.sum(col_acc, axis=0, keepdims=True)
    send_small(0, col_parts, r, [(i, {"row": i}) for i in range(4)])
    others(0, 1)
    row_sums = jnp.sum(lanes[...].T, axis=0, keepdims=True)
    old = decay_rate * col_old[:, mine]
    whole(0, col_parts, near).wait_recv()
    col_mine = old + (1.0 - decay_rate) * (total(col_parts) / rows_all + eps_one)
    inverse = 1.0 / col_mine

    def raw_step(k, _):
        span = pl.ds(pl.multiple_of(k * 8, 8), 8)
        g = full[y, span]
        sq = g * g * inverse
        part = sq[:, :128]
        for j in range(1, width // 128):
            part = part + sq[:, j * 128:(j + 1) * 128]
        lanes[span] = part
        return 0

    lax.fori_loop(0, rows // 8, raw_step, 0, unroll=4)
    raw_sums = jnp.sum(lanes[...].T, axis=0, keepdims=True)
    sums_yx[y * 4 + x] = jnp.concatenate([row_sums, raw_sums, weight_sums, jnp.zeros((1, 128), f32)], axis=0)
    send_small(1, sums_yx, y * 4 + x, [(i * 4 + j, {"dp": i, "col": j * 4 + z}) for i in range(4) for j in range(4)])
    others(1, PIECES[PX])
    for k in range(PIECES[PE]):
        for d in range(2):
            arrive(PD, d, k)
            bulk(PE, d, k).start()
    col_all[:, mine] = col_mine
    for q in (right, left, opp):
        pltpu.make_async_remote_copy(
            src_ref=col_all.at[:, mine], dst_ref=col_all.at[:, mine], send_sem=xs_sem.at[3],
            recv_sem=xr_sem.at[3], device_id={"dp": q}, device_id_type=MESH).start()
    whole(1, sums_yx, {"dp": right}).wait_recv()
    sums_zr[place] = jnp.concatenate([total(sums_yx)[0:3], row_old], axis=0)
    send_small(2, sums_zr, place, [(i * 4 + j, {"col": x * 4 + i, "row": j}) for i in range(4) for j in range(4)])
    cols_rest = col_all.at[:, pl.ds(0, 3 * width)]
    cols = pltpu.make_async_remote_copy(
        src_ref=cols_rest, dst_ref=cols_rest, send_sem=xs_sem.at[3], recv_sem=xr_sem.at[3],
        device_id={"dp": right}, device_id_type=MESH)
    cols.wait()
    col_scale[...] = lax.rsqrt(col_all[...])
    whole(0, col_parts, near).wait_send()
    whole(1, sums_yx, {"dp": right}).wait_send()
    for phase in (PB, PC, PD, PX):
        sent(phase)
    for k in range(PIECES[PX]):
        for d in range(2):
            arrive(PX, d, k)
    last = PIECES[PE] - 1
    for k in range(last):
        for d in range(2):
            bulk(PE, d, k).wait_send()
            arrive(PE, d, k)
    whole(2, sums_zr, near).wait_recv()

    def moments(group):
        tile = sums_zr[group]
        for i in range(1, 4):
            tile = tile + sums_zr[i * 4 + group]
        return tile, (decay_rate * 0.25) * tile[3:4] + (1.0 - decay_rate) * (tile[0:1] / cols_all + eps_one)

    _, row_mine = moments(r)
    row_new[...] = row_mine
    row_scale[...] = jnp.broadcast_to(lax.rsqrt(row_mine), (128, 128)).T
    sums = [jnp.zeros((1, 128), f32)] * 3
    for group in range(4):
        tile, row_one = moments(group)
        for i, part in enumerate((tile[1:2] / row_one, row_one, tile[2:3])):
            sums[i] = sums[i] + part
    sums = jnp.sum(jnp.concatenate(sums, axis=0), axis=1, keepdims=True)
    row_mean = sums[1:2] / rows_all
    clip = jnp.maximum(1.0, jnp.sqrt(sums[0:1] * row_mean / entries) / clip_level)
    size = learn_rate * jnp.maximum(eps_two, jnp.sqrt(sums[2:3] / entries))
    scal[...] = jnp.concatenate(
        [jnp.broadcast_to(v, (1, 128)) for v in (clip, size, jnp.sqrt(row_mean) / clip, clip)], axis=0)
    for d in range(2):
        bulk(PE, d, last).wait_send()
        arrive(PE, d, last)
    whole(2, sums_zr, near).wait_send()


def update_kernel(full, held, col_all, row_new, row_scale, col_scale, scal,
                  weight_out, update_out, row_out, col_out, clip_out,
                  new_weight, update, row_flat, col_flat, clip_flat, sem, small_sem):
    rows, width = full.shape[1], full.shape[2]
    row_flat[...] = row_new[...].reshape(row_flat.shape)
    col_flat[...] = col_all[...].reshape(col_flat.shape)
    clip_flat[...] = scal[0:1, 0:1]
    size, factor = scal[1:2, :], scal[2:3, :]
    step = 16
    copies = [pltpu.make_async_copy(src, dst, small_sem.at[i]) for i, (src, dst) in enumerate(
        ((row_flat, row_out), (col_flat, col_out), (clip_flat, clip_out)))]
    for copy in copies:
        copy.start()
    for k in range(rows // step):
        for i in range(step // 8):
            at = pl.ds(k * step + i * 8, 8)
            by_row = row_scale[at] * factor
            for q in range(4):
                for j in range(width // 128):
                    col = pl.ds(j * 128, 128)
                    out = pl.ds(q * width + j * 128, 128)
                    u = full[q, at, col] * by_row * col_scale[:, out]
                    update[at, out] = u
                    new_weight[at, out] = held[q, at, col] - size * u
        at = pl.ds(k * step, step)
        for which, (src, dst) in enumerate(((update, update_out), (new_weight, weight_out))):
            copies.append(pltpu.make_async_copy(src.at[at], dst.at[at], sem.at[which, k]))
            copies[-1].start()
    for copy in copies:
        copy.wait()


def solution(mesh):
    assert all(mesh.shape[axis] == size for axis, size in (("dp", 4), ("row", 4), ("col", 16)))

    def body(weight, grad_parts, row_moment, col_moment):
        rows, cols = weight.shape
        width = cols // 4
        vmem = pl.BlockSpec(memory_space=pltpu.VMEM)
        hbm = pl.BlockSpec(memory_space=pltpu.HBM)
        shapes = ((4, rows, width), (4, rows, width), (1, cols), (1, rows), (rows, 128), (1, cols), (4, 128))
        outs = pl.pallas_call(
            functools.partial(exchange_kernel, (rows * 4, cols * 16)),
            out_shape=tuple(pltpu.VMEM(s, f32) for s in shapes),
            in_specs=[hbm] * 4,
            out_specs=(vmem,) * len(shapes),
            scratch_shapes=[
                pltpu.VMEM((4, rows, width), jnp.bfloat16),
                *[pltpu.VMEM((rows, width), f32) for _ in range(6)],
                pltpu.VMEM((rows, 128), f32),
                pltpu.VMEM((rows,), f32),
                pltpu.VMEM((cols,), f32),
                pltpu.VMEM((1, cols), f32),
                pltpu.VMEM((4, 1, width), f32),
                pltpu.VMEM((16, 4, 128), f32),
                pltpu.VMEM((16, 4, 128), f32),
                pltpu.SemaphoreType.DMA((13,)),
                pltpu.SemaphoreType.DMA((6, 2, max(PIECES))),
                pltpu.SemaphoreType.DMA((6, 2, max(PIECES))),
                pltpu.SemaphoreType.DMA((4,)),
                pltpu.SemaphoreType.DMA((4,)),
                pltpu.SemaphoreType.REGULAR((2,)),
            ],
            compiler_params=pltpu.CompilerParams(
                collective_id=0, has_side_effects=True, vmem_limit_bytes=24 << 20),
            name="exchange",
        )(*(pltpu.with_memory_space_constraint(a, pltpu.HBM) for a in (grad_parts, weight, row_moment, col_moment)))
        new_weight, update, row_new, col_new, clip = pl.pallas_call(
            update_kernel,
            out_shape=(
                jax.ShapeDtypeStruct((rows, cols), f32),
                jax.ShapeDtypeStruct((rows, cols), f32),
                jax.ShapeDtypeStruct((rows,), f32),
                jax.ShapeDtypeStruct((cols,), f32),
                jax.ShapeDtypeStruct((1, 1), f32),
            ),
            in_specs=[vmem] * len(shapes),
            out_specs=(pl.BlockSpec(memory_space=pl.ANY),) * 5,
            scratch_shapes=[
                pltpu.VMEM((rows, cols), f32),
                pltpu.VMEM((rows, cols), f32),
                pltpu.VMEM((rows,), f32),
                pltpu.VMEM((cols,), f32),
                pltpu.VMEM((1, 1), f32),
                pltpu.SemaphoreType.DMA((2, rows // 16)),
                pltpu.SemaphoreType.DMA((3,)),
            ],
            compiler_params=pltpu.CompilerParams(vmem_limit_bytes=24 << 20),
            name="apply",
        )(*outs)
        return new_weight, update, row_new, col_new, clip.reshape(())

    return jax.shard_map(
        body,
        mesh=mesh,
        in_specs=(P("row", "col"), P("dp", "row", "col"), P("row"), P("col")),
        out_specs=(P("row", "col"), P("row", "col"), P("row"), P("col"), P()),
        check_vma=False,
    )
```

```python
import functools

import jax
import jax.numpy as jnp
from jax import lax
from jax.experimental import pallas as pl
from jax.experimental.pallas import tpu as pltpu
from jax.sharding import PartitionSpec as P

decay_rate = 0.5
eps_one = 1e-30
eps_two = 0.001
learn_rate = 0.01
clip_level = 1.0

MESH = pl.DeviceIdType.MESH
f32 = jnp.float32
PA, PB, PC, PD, PX, PE = range(6)
EARLY = 24
PIECES = (2, 1, 2, 2, 2, 2)


def exchange_kernel(sizes, grad_hbm, weight_hbm, rowm_hbm, colm_hbm,
                    full, held, col_all, row_new, row_scale, col_scale, scal,
                    own, s_opp, s_right, s_left, r_opp, r_left, r_right, lanes,
                    rowm, colm, col_old, col_parts, sums_yx, sums_zr,
                    load_sem, send_sem, recv_sem, xs_sem, xr_sem, ready):
    rows_all, cols_all = sizes
    rows, width = own.shape[1], own.shape[2]
    half = rows // 2
    entries = float(rows_all) * float(cols_all)
    y, r, c = lax.axis_index("dp"), lax.axis_index("row"), lax.axis_index("col")
    x, z = c // 4, lax.rem(c, 4)
    right, opp, left = lax.rem(y + 1, 4), lax.rem(y + 2, 4), lax.rem(y + 3, 4)

    loads = {}
    def first_rows(i):
        step = half // PIECES[PA]
        return pl.ds((i % 2) * half + (0 if i < 2 else step), step if i < 2 else half - step)

    cols = pl.ds(pl.multiple_of(opp * width, 128), width)
    firsts = [pltpu.make_async_copy(
        grad_hbm.at[0, first_rows(i), cols], own.at[2, first_rows(i)], load_sem.at[(2, 10, 11, 12)[i]]) for i in range(4)]
    for slot, q in ((1, right), (3, left), (0, y)):
        loads[slot] = pltpu.make_async_copy(
            grad_hbm.at[0, :, pl.ds(pl.multiple_of(q * width, 128), width)], own.at[slot], load_sem.at[slot])
    for q in range(4):
        loads[4 + q] = pltpu.make_async_copy(
            weight_hbm.at[:, pl.ds(q * width, width)], held.at[q], load_sem.at[4 + q])
    loads[8] = pltpu.make_async_copy(rowm_hbm, rowm, load_sem.at[8])
    loads[9] = pltpu.make_async_copy(colm_hbm, colm, load_sem.at[9])

    barrier = pltpu.get_barrier_semaphore()
    place = z * 4 + r
    hub = 1
    behind = lax.rem(place + 16 - hub, 16)

    def along_x(sem):
        for i in range(1, 4):
            pl.semaphore_signal(sem, inc=1, device_id={"col": i * 4 + z}, device_id_type=MESH)

    def along_z(sem):
        for i in reversed(range(16)):
            if i != hub:
                pl.semaphore_signal(sem, inc=1, device_id={"col": x * 4 + i // 4, "row": i % 4}, device_id_type=MESH)

    def answer():
        @pl.when(x > 0)
        def _():
            pl.semaphore_signal(ready.at[0], inc=1, device_id={"col": z}, device_id_type=MESH)

        @pl.when(behind > 0)
        def _():
            pl.semaphore_signal(
                ready.at[1], inc=1, device_id={"col": x * 4 + hub // 4, "row": hub % 4}, device_id_type=MESH)

    def tell():
        @pl.when(x == 0)
        def _():
            pl.semaphore_wait(ready.at[0], 3)
            along_x(ready.at[0])

        @pl.when(behind == 0)
        def _():
            pl.semaphore_wait(ready.at[1], 15)
            along_z(ready.at[1])

    def told():
        @pl.when(x > 0)
        def _():
            pl.semaphore_wait(ready.at[0], 1)

        @pl.when(behind > 0)
        def _():
            pl.semaphore_wait(ready.at[1], 1)

    for q in (right, left):
        pl.semaphore_signal(barrier, inc=1, device_id={"dp": q}, device_id_type=MESH)
    for copy in firsts[:2]:
        copy.start()
    for copy in firsts[2:]:
        copy.start()
    pl.when(x == 0)(lambda: along_x(barrier))
    pl.when(behind == 0)(lambda: along_z(barrier))

    def at(phase, h, k):
        if phase == PX:
            return pl.ds(h * half + (0, EARLY)[k], (EARLY, half - EARLY)[k])
        step = half // PIECES[phase]
        return pl.ds(h * half + k * step, step)

    def bulk(phase, d, k=0):
        if phase == PA:
            src, dst = s_opp.at[at(phase, d, k)], r_opp.at[at(phase, d, k)]
        elif phase in (PB, PC):
            h = d if phase == PC else 1 - d
            src, dst = ((s_right, r_left), (s_left, r_right))[d]
            src, dst = src.at[at(phase, h, k)], dst.at[at(phase, h, k)]
        else:
            h = 1 - d if phase == PX else d
            q = y if phase != PE else (left, right)[d]
            src = dst = full.at[q, at(phase, h, k)]
        return pltpu.make_async_remote_copy(
            src_ref=src, dst_ref=dst, send_sem=send_sem.at[phase, d, k], recv_sem=recv_sem.at[phase, d, k],
            device_id={"dp": (right, left)[d]}, device_id_type=MESH)

    def arrive(phase, d, k=0):
        if phase < PD:
            bulk(phase, d, k).wait_recv()
            return
        h = 1 - d if phase == PX else d
        q = (left, right)[d] if phase != PE else opp
        ref = full.at[q, at(phase, h, k)]
        pltpu.make_async_remote_copy(
            src_ref=ref, dst_ref=ref, send_sem=send_sem.at[phase, d, k], recv_sem=recv_sem.at[phase, d, k],
            device_id={"dp": (right, left)[d]}, device_id_type=MESH).wait_recv()

    def sent(phase):
        for k in range(PIECES[phase]):
            for d in range(2):
                bulk(phase, d, k).wait_send()

    for k in range(PIECES[PA]):
        for copy in (firsts[:2], firsts[2:], (), ())[k]:
            copy.wait()
        for d in range(2):
            span = at(PA, d, k)
            s_opp[span] = own[2, span].astype(f32)
        if k == 0:
            pl.semaphore_wait(barrier, 2 + (x + 3) // 4 + (behind + 15) // 16)
        for d in range(2):
            bulk(PA, d, k).start()
    for i in (1, 3, 0, 4, 5, 6, 7, 8, 9):
        loads[i].start()
    loads[1].wait()
    loads[3].wait()
    for d, (dst, slot) in enumerate(((s_right, 1), (s_left, 3))):
        span = at(PB, 1 - d, 0)
        dst[span] = own[slot, span].astype(f32)
        bulk(PB, d).start()
    for i in (0, 4, 5, 6, 7, 8, 9):
        loads[i].wait()

    def weight_step(i, acc):
        w = held[y, pl.ds(pl.multiple_of(i * 8, 8), 8)]
        sq = w * w
        for j in range(width // 128):
            acc = acc + sq[:, j * 128:(j + 1) * 128]
        return acc

    w_lanes = lax.fori_loop(0, rows // 8, weight_step, jnp.zeros((8, 128), f32), unroll=2)
    weight_sums = jnp.sum(w_lanes, axis=0, keepdims=True)
    col_old[...] = colm[...].reshape(col_old.shape)
    mine = pl.ds(pl.multiple_of(y * width, 128), width)
    row_old = rowm[...].reshape(1, rows)
    for k in range(PIECES[PC]):
        for d, (dst, slot) in enumerate(((s_right, 1), (s_left, 3))):
            span = at(PC, d, k)
            arrive(PA, d, k)
            dst[span] = r_opp[span] + own[slot, span].astype(f32)
            bulk(PC, d, k).start()
    answer()
    sent(PA)
    tell()
    col_acc = jnp.zeros((8, width), f32)
    arrive(PB, 0)
    arrive(PB, 1)
    for k in range(PIECES[PC]):
        for d in range(2):
            span = at(PC, d, k)
            arrive(PC, d, k)
            g = own[0, span].astype(f32) + r_left[span] + r_right[span]
            full[y, span] = g
            bulk(PD, d, k).start()
            sq = g * g
            for i in range(sq.shape[0] // 8):
                col_acc = col_acc + sq[i * 8:(i + 1) * 8]
            part = sq[:, :128]
            for j in range(1, width // 128):
                part = part + sq[:, j * 128:(j + 1) * 128]
            lanes[span] = part

    def send_small(stage, parts, at, devs):
        ref = parts.at[at]
        for i, dev in devs:
            @pl.when(at != i)
            def _():
                pltpu.make_async_remote_copy(
                    src_ref=ref, dst_ref=ref, send_sem=xs_sem.at[stage], recv_sem=xr_sem.at[stage],
                    device_id=dev, device_id_type=MESH).start()

    def whole(stage, parts, dev):
        rest = parts.at[pl.ds(0, parts.shape[0] - 1)]
        return pltpu.make_async_remote_copy(
            src_ref=rest, dst_ref=rest, send_sem=xs_sem.at[stage], recv_sem=xr_sem.at[stage],
            device_id=dev, device_id_type=MESH)

    def total(parts):
        out = parts[0]
        for i in range(1, parts.shape[0]):
            out = out + parts[i]
        return out

    near = {"row": lax.rem(r + 1, 4)}
    told()

    def others(first, last):
        for k in range(first, last):
            for d in range(2):
                bulk(PX, d, k).start()

    col_parts[r] = jnp.sum(col_acc, axis=0, keepdims=True)
    send_small(0, col_parts, r, [(i, {"row": i}) for i in range(4)])
    others(0, 1)
    row_sums = jnp.sum(lanes[...].T, axis=0, keepdims=True)
    old = decay_rate * col_old[:, mine]
    whole(0, col_parts, near).wait_recv()
    col_mine = old + (1.0 - decay_rate) * (total(col_parts) / rows_all + eps_one)
    inverse = 1.0 / col_mine

    def raw_step(k, _):
        span = pl.ds(pl.multiple_of(k * 8, 8), 8)
        g = full[y, span]
        sq = g * g * inverse
        part = sq[:, :128]
        for j in range(1, width // 128):
            part = part + sq[:, j * 128:(j + 1) * 128]
        lanes[span] = part
        return 0

    lax.fori_loop(0, rows // 8, raw_step, 0, unroll=4)
    raw_sums = jnp.sum(lanes[...].T, axis=0, keepdims=True)
    sums_yx[y * 4 + x] = jnp.concatenate([row_sums, raw_sums, weight_sums, jnp.zeros((1, 128), f32)], axis=0)
    send_small(1, sums_yx, y * 4 + x, [(i * 4 + j, {"dp": i, "col": j * 4 + z}) for i in range(4) for j in range(4)])
    for k in range(PIECES[PE]):
        for d in range(2):
            arrive(PD, d, k)
            bulk(PE, d, k).start()
        if k == 0:
            others(1, PIECES[PX])
    col_all[:, mine] = col_mine
    for q in (right, left, opp):
        pltpu.make_async_remote_copy(
            src_ref=col_all.at[:, mine], dst_ref=col_all.at[:, mine], send_sem=xs_sem.at[3],
            recv_sem=xr_sem.at[3], device_id={"dp": q}, device_id_type=MESH).start()
    whole(1, sums_yx, {"dp": right}).wait_recv()
    sums_zr[place] = jnp.concatenate([total(sums_yx)[0:3], row_old], axis=0)
    send_small(2, sums_zr, place, [(i * 4 + j, {"col": x * 4 + i, "row": j}) for i in range(4) for j in range(4)])
    cols_rest = col_all.at[:, pl.ds(0, 3 * width)]
    cols = pltpu.make_async_remote_copy(
        src_ref=cols_rest, dst_ref=cols_rest, send_sem=xs_sem.at[3], recv_sem=xr_sem.at[3],
        device_id={"dp": right}, device_id_type=MESH)
    cols.wait()
    col_scale[...] = lax.rsqrt(col_all[...])
    whole(0, col_parts, near).wait_send()
    whole(1, sums_yx, {"dp": right}).wait_send()
    for phase in (PB, PC, PD, PX):
        sent(phase)
    for k in range(PIECES[PX]):
        for d in range(2):
            arrive(PX, d, k)
    last = PIECES[PE] - 1
    for k in range(last):
        for d in range(2):
            bulk(PE, d, k).wait_send()
            arrive(PE, d, k)
    whole(2, sums_zr, near).wait_recv()

    def moments(group):
        tile = sums_zr[group]
        for i in range(1, 4):
            tile = tile + sums_zr[i * 4 + group]
        return tile, (decay_rate * 0.25) * tile[3:4] + (1.0 - decay_rate) * (tile[0:1] / cols_all + eps_one)

    _, row_mine = moments(r)
    row_new[...] = row_mine
    row_scale[...] = jnp.broadcast_to(lax.rsqrt(row_mine), (128, 128)).T
    sums = [jnp.zeros((1, 128), f32)] * 3
    for group in range(4):
        tile, row_one = moments(group)
        for i, part in enumerate((tile[1:2] / row_one, row_one, tile[2:3])):
            sums[i] = sums[i] + part
    sums = jnp.sum(jnp.concatenate(sums, axis=0), axis=1, keepdims=True)
    row_mean = sums[1:2] / rows_all
    clip = jnp.maximum(1.0, jnp.sqrt(sums[0:1] * row_mean / entries) / clip_level)
    size = learn_rate * jnp.maximum(eps_two, jnp.sqrt(sums[2:3] / entries))
    scal[...] = jnp.concatenate(
        [jnp.broadcast_to(v, (1, 128)) for v in (clip, size, jnp.sqrt(row_mean) / clip, clip)], axis=0)
    for d in range(2):
        bulk(PE, d, last).wait_send()
        arrive(PE, d, last)
    whole(2, sums_zr, near).wait_send()


def update_kernel(full, held, col_all, row_new, row_scale, col_scale, scal,
                  weight_out, update_out, row_out, col_out, clip_out,
                  new_weight, update, row_flat, col_flat, clip_flat, sem, small_sem):
    rows, width = full.shape[1], full.shape[2]
    row_flat[...] = row_new[...].reshape(row_flat.shape)
    col_flat[...] = col_all[...].reshape(col_flat.shape)
    clip_flat[...] = scal[0:1, 0:1]
    size, factor = scal[1:2, :], scal[2:3, :]
    step = 16
    copies = [pltpu.make_async_copy(src, dst, small_sem.at[i]) for i, (src, dst) in enumerate(
        ((row_flat, row_out), (col_flat, col_out), (clip_flat, clip_out)))]
    for copy in copies:
        copy.start()
    for k in range(rows // step):
        for i in range(step // 8):
            at = pl.ds(k * step + i * 8, 8)
            by_row = row_scale[at] * factor
            for q in range(4):
                for j in range(width // 128):
                    col = pl.ds(j * 128, 128)
                    out = pl.ds(q * width + j * 128, 128)
                    u = full[q, at, col] * by_row * col_scale[:, out]
                    update[at, out] = u
                    new_weight[at, out] = held[q, at, col] - size * u
        at = pl.ds(k * step, step)
        for which, (src, dst) in enumerate(((update, update_out), (new_weight, weight_out))):
            copies.append(pltpu.make_async_copy(src.at[at], dst.at[at], sem.at[which, k]))
            copies[-1].start()
    for copy in copies:
        copy.wait()


def solution(mesh):
    assert all(mesh.shape[axis] == size for axis, size in (("dp", 4), ("row", 4), ("col", 16)))

    def body(weight, grad_parts, row_moment, col_moment):
        rows, cols = weight.shape
        width = cols // 4
        vmem = pl.BlockSpec(memory_space=pltpu.VMEM)
        hbm = pl.BlockSpec(memory_space=pltpu.HBM)
        shapes = ((4, rows, width), (4, rows, width), (1, cols), (1, rows), (rows, 128), (1, cols), (4, 128))
        outs = pl.pallas_call(
            functools.partial(exchange_kernel, (rows * 4, cols * 16)),
            out_shape=tuple(pltpu.VMEM(s, f32) for s in shapes),
            in_specs=[hbm] * 4,
            out_specs=(vmem,) * len(shapes),
            scratch_shapes=[
                pltpu.VMEM((4, rows, width), jnp.bfloat16),
                *[pltpu.VMEM((rows, width), f32) for _ in range(6)],
                pltpu.VMEM((rows, 128), f32),
                pltpu.VMEM((rows,), f32),
                pltpu.VMEM((cols,), f32),
                pltpu.VMEM((1, cols), f32),
                pltpu.VMEM((4, 1, width), f32),
                pltpu.VMEM((16, 4, 128), f32),
                pltpu.VMEM((16, 4, 128), f32),
                pltpu.SemaphoreType.DMA((13,)),
                pltpu.SemaphoreType.DMA((6, 2, max(PIECES))),
                pltpu.SemaphoreType.DMA((6, 2, max(PIECES))),
                pltpu.SemaphoreType.DMA((4,)),
                pltpu.SemaphoreType.DMA((4,)),
                pltpu.SemaphoreType.REGULAR((2,)),
            ],
            compiler_params=pltpu.CompilerParams(
                collective_id=0, has_side_effects=True, vmem_limit_bytes=24 << 20),
            name="exchange",
        )(*(pltpu.with_memory_space_constraint(a, pltpu.HBM) for a in (grad_parts, weight, row_moment, col_moment)))
        new_weight, update, row_new, col_new, clip = pl.pallas_call(
            update_kernel,
            out_shape=(
                jax.ShapeDtypeStruct((rows, cols), f32),
                jax.ShapeDtypeStruct((rows, cols), f32),
                jax.ShapeDtypeStruct((rows,), f32),
                jax.ShapeDtypeStruct((cols,), f32),
                jax.ShapeDtypeStruct((1, 1), f32),
            ),
            in_specs=[vmem] * len(shapes),
            out_specs=(pl.BlockSpec(memory_space=pl.ANY),) * 5,
            scratch_shapes=[
                pltpu.VMEM((rows, cols), f32),
                pltpu.VMEM((rows, cols), f32),
                pltpu.VMEM((rows,), f32),
                pltpu.VMEM((cols,), f32),
                pltpu.VMEM((1, 1), f32),
                pltpu.SemaphoreType.DMA((2, rows // 16)),
                pltpu.SemaphoreType.DMA((3,)),
            ],
            compiler_params=pltpu.CompilerParams(vmem_limit_bytes=24 << 20),
            name="apply",
        )(*outs)
        return new_weight, update, row_new, col_new, clip.reshape(())

    return jax.shard_map(
        body,
        mesh=mesh,
        in_specs=(P("row", "col"), P("dp", "row", "col"), P("row"), P("col")),
        out_specs=(P("row", "col"), P("row", "col"), P("row"), P("col"), P()),
        check_vma=False,
    )
```
